512 devices in a mesh: dp: 16 (over z, y_hi), seq: 8 (over y_lo, core), tensor: 4 (over x).
Axes of the slice: x: 4, y: 8 (y_hi: 2, y_lo: 4; y = y_hi * 4 + y_lo), z: 8, core: 2. Of those that a mesh axis runs over, the one named last changes fastest.
Arguments:
- activations: bfloat16 [32768, 512], P(('dp', 'seq')), may hold values from -6 to 6
- d_logits: bfloat16 [32768, 8192], P(('dp', 'seq'), 'tensor'), may hold values from -0.015625 to 0.015625
- block_owner: int32 [16], replicated, may hold values from 0 to 15, each once
- left_stat: float32 [16, 512, 512], P('dp', ('seq', 'tensor')), may hold values from -0.1 to 2.1
- right_stat: float32 [16, 512, 512], P('dp', ('seq', 'tensor')), may hold values from -0.1 to 2.1
- second_moment: float32 [16, 512, 512], P('dp', ('seq', 'tensor')), may hold values from 2e-05 to 0.002
- left_root: float32 [16, 512, 512], P('dp', ('seq', 'tensor')), may hold values from -0.15 to 14
- right_root: float32 [16, 512, 512], P('dp', ('seq', 'tensor')), may hold values from -0.15 to 14
Outputs:
- update: bfloat16 [16, 512, 512], P(None, ('seq', 'tensor'))
- left_new: float32 [16, 512, 512], P('dp', ('seq', 'tensor'))
- right_new: float32 [16, 512, 512], P('dp', ('seq', 'tensor'))
- moment_new: float32 [16, 512, 512], P('dp', ('seq', 'tensor'))
The draws below stay inside these ranges and needn't reach their ends.
All inputs are finite; a program needn't handle non-finite values.
Results may differ from the reference program's by a relative error of at most 0.00055.
Values may be sent and summed in bfloat16 or wider, within the bound.
A program may use at most 64 MiB of HBM per device.

```python
import math
import jax
import jax.numpy as jnp
from jax import lax

BLK = 512
TOKENS = 32768
NBLK = 16
VW = 8192
BR = 128
RS = 16
N_SEQ = 8
N_TENSOR = 4


def symmetric_blocks(key, diag_lo, diag_hi, spread, rise):
    key_diag, key_off = jax.random.split(key)
    position = jnp.arange(BLK, dtype=jnp.float32) / BLK
    slope = math.log(rise)
    noise = jax.random.truncated_normal(key_off, -4.0, 4.0, (NBLK, BLK, BLK), jnp.float32)
    diagonal = jnp.exp(jax.random.uniform(key_diag, (NBLK, BLK), jnp.float32, math.log(diag_lo), math.log(diag_hi)))
    diagonal = diagonal * jnp.exp(slope * position)[None, :]
    symmetric = 0.5 * spread * (noise + jnp.swapaxes(noise, 1, 2))
    return symmetric + diagonal[:, :, None] * jnp.eye(BLK, dtype=jnp.float32)[None, :, :]


def draw_left_stat(key, part):
    return symmetric_blocks(jax.random.fold_in(key, 101), 0.5, 2.0, 0.02, 1.0)


def draw_right_stat(key, part):
    return symmetric_blocks(jax.random.fold_in(key, 102), 0.5, 2.0, 0.02, 1.0)


def draw_left_root(key, part):
    return symmetric_blocks(jax.random.fold_in(key, 103), 0.5, 1.5, 0.03, 3.0)


def draw_right_root(key, part):
    return symmetric_blocks(jax.random.fold_in(key, 104), 0.5, 1.5, 0.03, 3.0)


def draw_second_moment(key, part):
    folded = jax.random.fold_in(key, 105)
    position = jnp.arange(BLK, dtype=jnp.float32) / BLK
    falling = jnp.exp(-math.log(9.0) * position)[None, :, None]
    base_value = jnp.exp(jax.random.uniform(folded, (NBLK, BLK, BLK), jnp.float32, math.log(0.0002), math.log(0.002)))
    return base_value * falling


def raised(result, stream_key, source, target, parts, factor):
    owner, partner = [(jnp.arange(result.shape[axis_at]) // (result.shape[axis_at] // parts)).reshape([-1 if axis == axis_at else 1 for axis in range(result.ndim)]) for axis_at in (source, target)]
    chosen = jax.random.permutation(stream_key, parts)[partner]
    strong = (owner == chosen) | (owner == (partner + parts // 2) % parts)
    return jnp.where(strong, factor * result, result)


def levels(rng, shape, cuts, least, top_value):
    def one(dim, shards_of):
        steps = jax.random.uniform(jax.random.fold_in(jax.random.fold_in(rng, 6), dim), (shards_of,), jnp.float32, least / len(cuts), top_value / len(cuts))
        return jnp.repeat(jnp.exp(steps), shape[dim] // shards_of).reshape((-1,) + (1,) * (len(shape) - dim - 1))

    level = one(*cuts[0])
    for cut in cuts[1:]:
        level = level * one(*cut)
    return level


def bell_draw(own_key, dims, width, bound, shards=(), kind=jnp.bfloat16):
    values = jax.random.normal(own_key, dims, jnp.float32) * width
    if len(shards) > 0:
        values = levels(own_key, dims, shards, -0.22, 0.18) * values
    return jnp.clip(values, min=-bound, max=bound).astype(kind)


def bell_draw_with(own_key, shape, deviation, bound, cuts, heavy, held_as=jnp.bfloat16):
    result = deviation * jax.random.normal(own_key, shape, jnp.float32)
    if cuts:
        result = result * levels(own_key, shape, cuts, -0.22, 0.18)
    return jnp.clip(raised(result, jax.random.fold_in(own_key, 3), *heavy), -bound, bound).astype(held_as)


def setup_inputs(seed: int = 0) -> dict:
    keys = jax.random.split(jax.random.key(seed), 9)
    return {
        "activations": bell_draw(keys[0], (TOKENS, BLK), 1.0, 6.0, ((0, 128),)),
        "d_logits": bell_draw_with(keys[1], (TOKENS, VW), (0.05 * TOKENS ** -0.5), 0.015625, ((0, 128), (1, 4)), (0, 1, 128, 5.5)),
        "block_owner": jax.random.permutation(keys[2], NBLK).astype(jnp.int32),
        "left_stat": draw_left_stat(jax.random.fold_in(keys[8], 71), 0),
        "right_stat": draw_right_stat(jax.random.fold_in(keys[8], 71), 0),
        "second_moment": draw_second_moment(jax.random.fold_in(keys[8], 71), 0),
        "left_root": draw_left_root(jax.random.fold_in(keys[8], 71), 0),
        "right_root": draw_right_root(jax.random.fold_in(keys[8], 71), 0),
    }


highest = lax.Precision.HIGHEST

def reference(activations, d_logits, block_owner, left_stat, right_stat, second_moment, left_root, right_root):
    gradient = lax.dot_general(d_logits, activations, (((0,), (0,)), ((), ())), preferred_element_type=jnp.float32)
    blocks = gradient.reshape(N_TENSOR, NBLK, BR, BLK).reshape(N_TENSOR, NBLK, N_SEQ, RS, BLK)
    blocks = blocks.transpose(1, 2, 0, 3, 4).reshape(NBLK, BLK, BLK)
    owner_block = jnp.zeros((NBLK,), jnp.int32).at[block_owner].set(jnp.arange(NBLK, dtype=jnp.int32))
    owned_blocks = blocks[owner_block]

    def per_owner(operands):
        grad_block, left_old, right_old, moment_old, left_factor, right_factor = operands
        left_next = 0.95 * left_old + jnp.dot(grad_block, grad_block.T, precision=highest, preferred_element_type=jnp.float32)
        right_next = 0.95 * right_old + jnp.dot(grad_block.T, grad_block, precision=highest, preferred_element_type=jnp.float32)
        moment_next = 0.99 * moment_old + 0.01 * grad_block * grad_block
        adam_dir = grad_block / (jnp.sqrt(moment_next) + 1e-08)
        mixed_rows = jnp.dot(left_factor, grad_block, precision=highest, preferred_element_type=jnp.float32)
        precond = jnp.dot(mixed_rows, right_factor, precision=highest, preferred_element_type=jnp.float32)
        graft_scale = jnp.sqrt(jnp.sum(adam_dir * adam_dir)) / (jnp.sqrt(jnp.sum(precond * precond)) + 1e-06)
        return ((graft_scale * precond).astype(jnp.bfloat16), left_next, right_next, moment_next)
    updates, left_new, right_new, moment_new = lax.map(per_owner, (owned_blocks, left_stat, right_stat, second_moment, left_root, right_root))
    update = updates[block_owner]
    return (update, left_new, right_new, moment_new)
```

```python
import jax
import jax.numpy as jnp
from jax import lax
from jax.experimental import pallas as pl
from jax.experimental.pallas import tpu as pltpu
from jax.sharding import PartitionSpec as P

F32 = jnp.float32
BF16 = jnp.bfloat16
MESH = pl.DeviceIdType.MESH

NZ = 8
NY = 8
NL = 4
NX = 4
PIECES = 4
PIECE_ORDER = ((2, 3, 0, 1), (0, 1, 2, 3))


def split(value):
    high = value.astype(BF16)
    return high, (value - high.astype(F32)).astype(BF16)


def dot(a, b):
    return jnp.dot(a, b, preferred_element_type=F32)


def dot_nt(a, b):
    return lax.dot_general(a, b, (((1,), (1,)), ((), ())), preferred_element_type=F32)


def dot_tn(a, b):
    return lax.dot_general(a, b, (((0,), (0,)), ((), ())), preferred_element_type=F32)


def sum_all(value):
    return jnp.sum(jnp.sum(value, axis=0, keepdims=True), axis=1, keepdims=True)


def kernel(
    owner_ref, owned_ref, acts_ref, logit_ref, left_ref, right_ref, moment_ref, lroot_ref, rroot_ref,
    update_out, left_out, right_out, moment_out,
    logit_own, logit_other, acts_other, part, ring_in, axis_in, grad, rroot, grad_hi, grad_lo,
    rroot_hi, rroot_lo, columns, norms, updates,
    load_done, ex_send, ex_recv, ring_send, ring_recv, axis_send, axis_recv, gather_send, gather_recv,
    norm_send, norm_recv, update_send, update_recv,
):
    dp = lax.axis_index("dp")
    seq = lax.axis_index("seq")
    x = lax.axis_index("tensor")
    z, yh = dp // 2, dp % 2
    yl, c = seq // 2, seq % 2
    y = yh * NL + yl
    half = acts_ref.shape[1] // 2

    def at_yz(y_to, z_to):
        return (z_to * 2 + y_to // NL, (y_to % NL) * 2 + c, x)

    def in_group(yl_to, c_to, x_to):
        return (dp, yl_to * 2 + c_to, x_to)

    sibling = in_group(yl, 1 - c, x)
    i = (1 - c) * z + c * y
    me2 = (1 - c) * y + c * z

    def on_first(k):
        return at_yz((1 - c) * y + c * k, (1 - c) * k + c * z)

    def on_second(k):
        return at_yz((1 - c) * k + c * y, (1 - c) * z + c * k)

    ring_next = on_first((i + 1) % 8)
    ring_prev = on_first((i + 7) % 8)
    x_next, x_prev, x_far = (x + 1) % NX, (x + 3) % NX, (x + 2) % NX

    for b in range(owner_ref.shape[0]):
        band = logit_ref.shape[1] // owner_ref.shape[0]
        pltpu.make_async_copy(logit_ref.at[:, pl.ds(b * band, band)], logit_own.at[b], load_done).start()

    barrier = pltpu.get_barrier_semaphore()

    def signal(device):
        pl.semaphore_signal(barrier, inc=1, device_id=device, device_id_type=MESH)

    partners = 0
    for dx in range(NX):
        for dy in range(NL):
            for dc in range(2):
                if dx or dy or dc:
                    signal(in_group((yl + dy) % NL, (c + dc) % 2, (x + dx) % NX))
                    partners += 1
    for k in range(NL):
        signal(at_yz((1 - yh) * NL + k, z))
        partners += 1
    for k in range(1, NZ):
        signal(at_yz(y, (z + k) % NZ))
        partners += 1
    pl.semaphore_wait(barrier, partners)

    def remote(src, dst, send, recv, device):
        return pltpu.make_async_remote_copy(
            src_ref=src, dst_ref=dst, send_sem=send, recv_sem=recv,
            device_id=device, device_id_type=MESH,
        )

    blocks = owner_ref.shape[0]
    band = logit_ref.shape[1] // blocks
    exchange = [
        remote(
            acts_ref.at[:, pl.ds(pl.multiple_of((1 - c) * half, half), half)],
            acts_other, ex_send.at[0], ex_recv.at[0], sibling,
        )
    ]
    exchange[0].start()
    for b in range(blocks):
        strip = logit_ref.at[:, pl.ds(b * band, band)]
        remote(strip, logit_other.at[b], ex_send.at[1], ex_recv.at[1], sibling).start()
    exchange.append(remote(logit_other, logit_other, ex_send.at[1], ex_recv.at[1], sibling))

    def gather(which, slab):
        sent = []

        def arrive(q, core, column):
            place = slab(q, core, column)
            remote(
                place, place, gather_send.at[which, 0], gather_recv.at[which, core, q, column], sibling
            ).wait_recv()

        def push(q, column, device):
            place = slab(q, c, column)
            copy = remote(
                place, place, gather_send.at[which, len(sent)],
                gather_recv.at[which, c, q, column], device,
            )
            copy.start()
            sent.append(copy)

        to_next, to_prev = in_group(yl, c, x_next), in_group(yl, c, x_prev)

        def begin():
            push(yl, x, to_next)
            push(yl, x, to_prev)
            for dy in range(1, NL):
                push(yl, x, in_group((yl + dy) % NL, c, x))
            push(yl, x, sibling)

        def middle():
            arrive(yl, c, x_prev)
            push(yl, x_prev, to_next)
            push(yl, x_prev, sibling)
            arrive(yl, c, x_next)
            push(yl, x_next, sibling)
            for dy in range(1, NL):
                q = (yl + NL - dy) % NL
                arrive(q, c, x)
                push(q, x, to_next)
                push(q, x, to_prev)
                push(q, x, sibling)

        def late():
            for dy in range(1, NL):
                q = (yl + NL - dy) % NL
                arrive(q, c, x_prev)
                if dy == 1:
                    push(q, x_prev, to_next)
                push(q, x_prev, sibling)
                arrive(q, c, x_next)
                if dy >= 2:
                    push(q, x_next, to_prev)
                push(q, x_next, sibling)

        def end():
            for dy in range(NL):
                q = (yl + NL - dy) % NL
                arrive(q, c, x_far)
                push(q, x_far, sibling)
            for dx in range(NX):
                for dy in range(NL):
                    arrive((yl + dy) % NL, 1 - c, (x + dx) % NX)

        return begin, middle, late, end, sent

    rroot[yl, c, x] = rroot_ref[0]
    r_begin, r_middle, r_late, r_end, r_sent = gather(0, lambda q, core, column: rroot.at[q, core, column])
    g_begin, g_middle, g_late, g_end, g_sent = gather(1, lambda q, core, column: grad.at[core, q, :, column])
    r_begin()

    unit = band // NL

    def place(d, q):
        row = (d % 2) * NL + q
        return (1 - c) * ((d // 2) * 8 + row) + c * (row * 8 + d // 2)

    acts_own = acts_ref[:, pl.ds(pl.multiple_of(c * half, half), half)]

    def own_block(d, carry):
        rows = dot_tn(logit_own[owned_ref[d]], acts_own)
        for q in range(NL):
            part[place(d, q)] = rows[q * unit : (q + 1) * unit]
        return carry

    pltpu.make_async_copy(logit_own, logit_own, load_done).wait()
    lax.fori_loop(0, blocks, own_block, 0)
    r_middle()
    for copy in exchange:
        copy.wait_recv()

    acts_rest = acts_other[...]

    def other_block(d, carry):
        rows = dot_tn(logit_other[owned_ref[d]], acts_rest)
        for q in range(NL):
            spot = place(d, q)
            part[spot] = part[spot] + rows[q * unit : (q + 1) * unit]
        return carry

    lax.fori_loop(0, blocks, other_block, 0)

    def chunk(way, step):
        return (i + 4 - step) % 8 if way == 0 else (i + 4 + step) % 8

    def ring(way, step, piece):
        return remote(
            part.at[pl.ds(chunk(way, step) * 8 + 2 * piece, 2)],
            ring_in.at[way, step, pl.ds(2 * piece, 2)],
            ring_send.at[way, step, piece], ring_recv.at[way, step, piece],
            (ring_next, ring_prev)[way],
        )

    def first_pieces(way):
        return (0, 1) if way == 0 else (2, 3)

    def ring_add(spot, way, step, piece):
        ring(way, step, piece).wait_recv()
        rows = pl.ds(spot * 8 + 2 * piece, 2)
        part[rows] = part[rows] + ring_in[way, step, pl.ds(2 * piece, 2)]

    for k in range(2):
        for way in range(2):
            ring(way, 0, first_pieces(way)[k]).start()
    for k in range(2):
        for way in range(2):
            ring(way, 1, PIECE_ORDER[way][k]).start()
    r_late()
    for step in range(1, 4):
        for k in range(PIECES):
            for way in range(2):
                piece = PIECE_ORDER[way][k]
                if step == 1 and k < 2:
                    continue
                ring_add(chunk(way, step), way, step - 1, piece)
                ring(way, step, piece).start()

    def axis_copy(j):
        return remote(
            part.at[i * 8 + j], axis_in.at[me2], axis_send.at[j], axis_recv.at[me2], on_second(j)
        )

    for k in range(PIECES):
        for way in range(2):
            ring_add(i, way, 3, PIECE_ORDER[way][k])
        for piece in {2: (0, 2), 3: (1, 3)}.get(k, ()):
            for j in (2 * piece, 2 * piece + 1):

                @pl.when(j != me2)
                def _():
                    axis_copy(j).start()

    r_end()
    value = rroot[...].reshape(rroot_hi.shape)
    rroot_hi[...], rroot_lo[...] = split(value)

    total = part[i * 8 + me2]
    for k in range(1, 8):
        j = (me2 + k) % 8
        remote(part.at[i * 8 + j], axis_in.at[j], axis_send.at[j], axis_recv.at[j], sibling).wait_recv()
        total = total + axis_in[j]
    grad[c, yl, :, x] = total.reshape(2, unit // 2, half)

    g_begin()
    g_middle()
    g_late()
    g_end()

    own = jnp.concatenate([grad[0, yl, c, x], grad[1, yl, c, x]], axis=1)
    moment = 0.99 * moment_ref[0] + 0.01 * own * own
    moment_out[0] = moment
    adam = own / (jnp.sqrt(moment) + 1e-08)
    adam_part = sum_all(adam * adam)

    for s in range(2):
        grad_hi[s], grad_lo[s] = split(grad[s].reshape(grad_hi.shape[1:]))

    def times_grad(value):
        rows = value.shape[0]
        high, low = split(value)
        both = jnp.concatenate([high, low], axis=0)
        out = []
        for s in range(2):
            wide = dot(both, grad_hi[s])
            out.append(wide[:rows] + (wide[rows:] + dot(high, grad_lo[s])))
        return jnp.concatenate(out, axis=1)

    mixed = times_grad(lroot_ref[0])
    mixed_hi, mixed_lo = split(mixed)
    wide = dot(jnp.concatenate([mixed_hi, mixed_lo], axis=0), rroot_hi[...])
    count = mixed.shape[0]
    precond = wide[:count] + (wide[count:] + dot(mixed_hi, rroot_lo[...]))
    precond_part = sum_all(precond * precond)

    lanes = norms.shape[2]
    rank = (yl * 2 + c) * NX + x
    norms[rank] = jnp.concatenate(
        [jnp.broadcast_to(adam_part, (1, lanes)), jnp.broadcast_to(precond_part, (1, lanes))], axis=0
    )
    for dx in range(NX):
        for dy in range(NL):
            for dc in range(2):
                if dx or dy or dc:
                    remote(
                        norms.at[rank], norms.at[rank], norm_send, norm_recv,
                        in_group((yl + dy) % NL, (c + dc) % 2, (x + dx) % NX),
                    ).start()

    own_hi, own_lo = split(own)
    both = jnp.concatenate([own_hi, own_lo], axis=0)
    outer = 0.95 * left_ref[0]
    for s in range(2):
        span = slice(s * half, (s + 1) * half)
        wide = dot_nt(both[:, span], grad_hi[s])
        outer = outer + (wide[:count] + (wide[count:] + dot_nt(own_hi[:, span], grad_lo[s])))
    left_out[0] = outer

    everyone = norms.at[pl.ds(0, norms.shape[0] - 1)]
    remote(everyone, everyone, norm_send, norm_recv, sibling).wait()
    sums = jnp.sum(norms[...], axis=0)
    scale = jnp.sqrt(sums[0:1, 0:1]) / (jnp.sqrt(sums[1:2, 0:1]) + 1e-06)
    updates[dp] = (scale * precond).astype(BF16)

    def update_copy(d, k, device):
        return remote(updates.at[d], updates.at[d], update_send.at[k], update_recv.at[d], device)

    across = z * 2 + (1 - yh)
    update_sent = [update_copy(dp, 0, at_yz((1 - yh) * NL + yl, z))]
    for k in range(1, NZ):
        update_sent.append(update_copy(dp, k, at_yz(y, (z + k) % NZ)))
    for copy in update_sent:
        copy.start()
    update_copy(across, 0, sibling).wait_recv()
    for k in range(1, NZ):
        copy = update_copy(across, NZ - 1 + k, at_yz(y, (z + k) % NZ))
        copy.start()
        update_sent.append(copy)

    first = seq * (NX * count) + x * count
    lane = 128
    side = first // half
    tile = grad_hi.shape[1]
    strip = grad[side, :, :, :, :, pl.ds(pl.multiple_of((first % half) // lane * lane, lane), lane)]
    columns[...] = strip.reshape(tile, lane).T
    picked = columns[pl.ds(pl.multiple_of(first % lane, count), count)]
    right_out[0] = 0.95 * right_ref[0] + times_grad(picked)

    for k in range(1, NZ):
        for side_y in range(2):
            update_copy(((z + k) % NZ) * 2 + side_y, 0, sibling).wait_recv()
    for b in range(blocks):
        update_out[b] = updates[owner_ref[b]]

    for copy in exchange:
        copy.wait_send()
    for way in range(2):
        for piece in first_pieces(way):
            ring(way, 0, piece).wait_send()
        for step in range(1, 4):
            for piece in range(PIECES):
                ring(way, step, piece).wait_send()
    for k in range(1, 8):
        axis_copy((me2 + k) % 8).wait_send()
    for copy in r_sent + g_sent + update_sent:
        copy.wait_send()


def per_device(
    activations, d_logits, block_owner, left_stat, right_stat, second_moment, left_root, right_root
):
    tokens, width = activations.shape
    blocks = block_owner.shape[0]
    half = width // 2
    indices = jnp.arange(blocks, dtype=jnp.int32)
    owned = jnp.sum(jnp.where(block_owner[None, :] == indices[:, None], indices[None, :], 0), axis=1)
    rows = left_stat.shape[1]
    unit = 2 * rows
    vmem = pl.BlockSpec(memory_space=pltpu.VMEM)
    smem = pl.BlockSpec(memory_space=pltpu.SMEM)
    dma = pltpu.SemaphoreType.DMA
    stat = jax.ShapeDtypeStruct(left_stat.shape, F32)
    return pl.pallas_call(
        kernel,
        out_shape=(jax.ShapeDtypeStruct((blocks, rows, width), BF16), stat, stat, stat),
        in_specs=[smem, smem, vmem, pl.BlockSpec(memory_space=pl.ANY)] + [vmem] * 5,
        out_specs=(vmem,) * 4,
        scratch_shapes=[
            pltpu.VMEM((blocks, tokens, d_logits.shape[1] // blocks), BF16),
            pltpu.VMEM((blocks, tokens, d_logits.shape[1] // blocks), BF16),
            pltpu.VMEM((tokens, half), BF16),
            pltpu.VMEM((64, unit, half), F32),
            pltpu.VMEM((2, 4, 8, unit, half), F32),
            pltpu.VMEM((8, unit, half), F32),
            pltpu.VMEM((2, NL, 2, NX, rows, half), F32),
            pltpu.VMEM((NL, 2, NX, rows, width), F32),
            pltpu.VMEM((2, width, half), BF16),
            pltpu.VMEM((2, width, half), BF16),
            pltpu.VMEM((width, width), BF16),
            pltpu.VMEM((width, width), BF16),
            pltpu.VMEM((128, width), F32),
            pltpu.VMEM((32, 2, 128), F32),
            pltpu.VMEM((blocks, rows, width), BF16),
            dma, dma((2,)), dma((2,)),
            dma((2, 4, PIECES)), dma((2, 4, PIECES)),
            dma((8,)), dma((8,)),
            dma((2, 34)), dma((2, 2, NL, NX)),
            dma, dma,
            dma((15,)), dma((16,)),
        ],
        compiler_params=pltpu.CompilerParams(
            collective_id=0, has_side_effects=True, vmem_limit_bytes=40 * 2**20
        ),
    )(block_owner, owned, activations, d_logits, left_stat, right_stat, second_moment, left_root, right_root)


def solution(mesh):
    shards = P("dp", ("seq", "tensor"), None)
    return jax.shard_map(
        per_device,
        mesh=mesh,
        in_specs=(P(("dp", "seq"), None), P(("dp", "seq"), "tensor"), P()) + (shards,) * 5,
        out_specs=(P(None, ("seq", "tensor"), None), shards, shards, shards),
        check_vma=False,
    )
```

```python
import jax
import jax.numpy as jnp
from jax import lax
from jax.experimental import pallas as pl
from jax.experimental.pallas import tpu as pltpu
from jax.sharding import PartitionSpec as P

F32 = jnp.float32
BF16 = jnp.bfloat16
MESH = pl.DeviceIdType.MESH

NZ = 8
NY = 8
NL = 4
NX = 4
PIECES = 4
PIECE_ORDER = ((2, 3, 0, 1), (0, 1, 2, 3))


def split(value):
    high = value.astype(BF16)
    return high, (value - high.astype(F32)).astype(BF16)


def dot(a, b):
    return jnp.dot(a, b, preferred_element_type=F32)


def dot_nt(a, b):
    return lax.dot_general(a, b, (((1,), (1,)), ((), ())), preferred_element_type=F32)


def dot_tn(a, b):
    return lax.dot_general(a, b, (((0,), (0,)), ((), ())), preferred_element_type=F32)


def sum_all(value):
    return jnp.sum(jnp.sum(value, axis=0, keepdims=True), axis=1, keepdims=True)


def kernel(
    owned_ref, acts_hbm, logit_ref, left_hbm, right_hbm, moment_hbm, lroot_hbm, rroot_hbm,
    updates, left_out, right_out, moment_out,
    acts_ref, left_ref, right_ref, moment_ref, lroot_ref, logit_own, logit_other, acts_other, part, ring_in, axis_in, grad, rroot, grad_hi, grad_lo,
    rroot_hi, rroot_lo, columns, norms,
    load_done, ex_send, ex_recv, ring_send, ring_recv, axis_send, axis_recv, gather_send, gather_recv,
    norm_send, norm_recv, update_send, update_recv,
):
    dp = lax.axis_index("dp")
    seq = lax.axis_index("seq")
    x = lax.axis_index("tensor")
    z, yh = dp // 2, dp % 2
    yl, c = seq // 2, seq % 2
    y = yh * NL + yl
    half = acts_ref.shape[1] // 2
    pending = []

    def at_yz(y_to, z_to):
        return (z_to * 2 + y_to // NL, (y_to % NL) * 2 + c, x)

    def in_group(yl_to, c_to, x_to):
        return (dp, yl_to * 2 + c_to, x_to)

    sibling = in_group(yl, 1 - c, x)
    i = (1 - c) * z + c * y
    me2 = (1 - c) * y + c * z

    def on_first(k):
        return at_yz((1 - c) * y + c * k, (1 - c) * k + c * z)

    def on_second(k):
        return at_yz((1 - c) * k + c * y, (1 - c) * z + c * k)

    ring_next = on_first((i + 1) % 8)
    ring_prev = on_first((i + 7) % 8)
    x_next, x_prev, x_far = (x + 1) % NX, (x + 3) % NX, (x + 2) % NX

    acts_load = pltpu.make_async_copy(acts_hbm, acts_ref, load_done.at[1])
    rroot_load = pltpu.make_async_copy(rroot_hbm.at[0], rroot.at[yl, c, x], load_done.at[2])
    stat_loads = [
        pltpu.make_async_copy(source, target, load_done.at[3 + k])
        for k, (source, target) in enumerate(
            ((left_hbm, left_ref), (right_hbm, right_ref), (moment_hbm, moment_ref), (lroot_hbm, lroot_ref))
        )
    ]
    rroot_load.start()
    acts_load.start()
    blocks = owned_ref.shape[0]
    band = logit_ref.shape[1] // blocks
    for b in range(blocks):
        pltpu.make_async_copy(logit_ref.at[:, pl.ds(b * band, band)], logit_own.at[b], load_done.at[0]).start()

    for load in stat_loads:
        load.start()

    barrier = pltpu.get_barrier_semaphore()

    def signal(device):
        pl.semaphore_signal(barrier, inc=1, device_id=device, device_id_type=MESH)

    partners = 0
    for dx in range(NX):
        for dy in range(NL):
            for dc in range(2):
                if dx or dy or dc:
                    signal(in_group((yl + dy) % NL, (c + dc) % 2, (x + dx) % NX))
                    partners += 1
    for k in range(NL):
        signal(at_yz((1 - yh) * NL + k, z))
        partners += 1
    for k in range(1, NZ):
        signal(at_yz(y, (z + k) % NZ))
        partners += 1
    pl.semaphore_wait(barrier, partners)

    def remote(src, dst, send, recv, device):
        return pltpu.make_async_remote_copy(
            src_ref=src, dst_ref=dst, send_sem=send, recv_sem=recv,
            device_id=device, device_id_type=MESH,
        )

    exchange = [
        remote(
            acts_hbm.at[:, pl.ds(pl.multiple_of((1 - c) * half, half), half)],
            acts_other, ex_send.at[0], ex_recv.at[0], sibling,
        )
    ]
    exchange[0].start()
    for b in range(blocks):
        strip = logit_ref.at[:, pl.ds(b * band, band)]
        remote(strip, logit_other.at[b], ex_send.at[1], ex_recv.at[1], sibling).start()
    exchange.append(remote(logit_other, logit_other, ex_send.at[1], ex_recv.at[1], sibling))

    def gather(which, slab, band_of):
        count = [0]

        def describe(place, k, core, q, column, device):
            return remote(
                place, place, gather_send.at[which, k], gather_recv.at[which, core, q, column], device
            )

        def arrive(q, column):
            describe(slab(q, c, column), 0, c, q, column, sibling).wait_recv()

        def launch(place, q, column, device):
            copy = describe(place, count[0], c, q, column, device)
            count[0] += 1
            copy.start()
            pending.append(copy)

        def push(q, column, device):
            launch(slab(q, c, column), q, column, device)

        def share(q):
            launch(band_of(q, c), q, 0, sibling)

        to_next, to_prev = in_group(yl, c, x_next), in_group(yl, c, x_prev)

        def around(k):
            return (yl, yl + 1 - 2 * (yl % 2), (yl + 2) % NL, NL - 1 - yl)[k]

        def begin():
            for dy in range(1, NL):
                push(yl, x, in_group(around(dy), c, x))
            push(yl, x, to_next)
            push(yl, x, to_prev)

        def middle():
            arrive(yl, x_prev)
            push(yl, x_prev, to_next)
            for dy in range(1, NL):
                arrive(around(dy), x)
                push(around(dy), x, to_next)
                push(around(dy), x, to_prev)

        def late():
            arrive(around(1), x_prev)
            push(around(1), x_prev, to_next)
            for dy in (2, 3):
                arrive(around(dy), x_next)
                push(around(dy), x_next, to_prev)

        def end():
            for dy in range(NL):
                q = around(dy)
                arrive(q, x_far)
                arrive(q, x_next if dy < 2 else x_prev)
                share(q)

        def finish():
            for q in range(NL):
                describe(band_of(q, 1 - c), 0, 1 - c, q, 0, sibling).wait_recv()

        return begin, middle, late, end, finish

    rroot_load.wait()
    r_begin, r_middle, r_late, r_end, r_finish = gather(
        0, lambda q, core, column: rroot.at[q, core, column], lambda q, core: rroot.at[q, core]
    )
    g_begin, g_middle, g_late, g_end, g_finish = gather(
        1, lambda q, core, column: grad.at[core, q, :, column], lambda q, core: grad.at[core, q]
    )
    r_begin()

    unit = band // NL

    def place(d, q):
        row = (d % 2) * NL + q
        return (1 - c) * ((d // 2) * 8 + row) + c * (row * 8 + d // 2)

    def own_block(d, carry):
        rows = dot_tn(logit_own[owned_ref[d]], acts_own)
        for q in range(NL):
            part[place(d, q)] = rows[q * unit : (q + 1) * unit]
        return carry

    pltpu.make_async_copy(logit_own, logit_own, load_done.at[0]).wait()
    acts_load.wait()
    acts_own = acts_ref[:, pl.ds(pl.multiple_of(c * half, half), half)]
    lax.fori_loop(0, blocks, own_block, 0, unroll=4)
    for copy in exchange:
        copy.wait_recv()
    pending.extend(exchange)

    acts_rest = acts_other[...]

    def other_block(d, carry):
        rows = dot_tn(logit_other[owned_ref[d]], acts_rest)
        for q in range(NL):
            spot = place(d, q)
            part[spot] = part[spot] + rows[q * unit : (q + 1) * unit]
        return carry

    lax.fori_loop(0, blocks, other_block, 0, unroll=4)

    def chunk(way, step):
        return (i + 4 - step) % 8 if way == 0 else (i + 4 + step) % 8

    def ring(way, step, piece):
        return remote(
            part.at[pl.ds(chunk(way, step) * 8 + 2 * piece, 2)],
            ring_in.at[way, step, pl.ds(2 * piece, 2)],
            ring_send.at[way, step, piece], ring_recv.at[way, step, piece],
            (ring_next, ring_prev)[way],
        )

    def first_pieces(way):
        return (0, 1) if way == 0 else (2, 3)

    def ring_add(spot, way, step, piece):
        ring(way, step, piece).wait_recv()
        rows = pl.ds(spot * 8 + 2 * piece, 2)
        part[rows] = part[rows] + ring_in[way, step, pl.ds(2 * piece, 2)]

    def ring_send_off(way, step, piece):
        copy = ring(way, step, piece)
        copy.start()
        pending.append(copy)

    for k in range(2):
        for way in range(2):
            ring_send_off(way, 0, first_pieces(way)[k])
    for k in range(2):
        for way in range(2):
            ring_send_off(way, 1, PIECE_ORDER[way][k])
    r_middle()
    for step in range(1, 4):
        if step == 2:
            r_late()
        if step == 3:
            r_end()
        for k in range(PIECES):
            for way in range(2):
                piece = PIECE_ORDER[way][k]
                if step == 1 and k < 2:
                    continue
                ring_add(chunk(way, step), way, step - 1, piece)
                ring_send_off(way, step, piece)

    def axis_copy(j):
        return remote(
            part.at[i * 8 + j], axis_in.at[me2], axis_send.at[j], axis_recv.at[me2], on_second(j)
        )

    for k in range(PIECES):
        for way in range(2):
            ring_add(i, way, 3, PIECE_ORDER[way][k])
        for piece in {2: (0, 2), 3: (1, 3)}.get(k, ()):
            for j in (2 * piece, 2 * piece + 1):

                @pl.when(j != me2)
                def _():
                    axis_copy(j).start()

    for k in range(1, 8):
        pending.append(axis_copy((me2 + k) % 8))
    r_finish()
    value = rroot[...].reshape(rroot_hi.shape)
    rroot_hi[...], rroot_lo[...] = split(value)

    total = part[i * 8 + me2]
    for k in range(1, 8):
        j = (me2 + k) % 8
        remote(part.at[i * 8 + j], axis_in.at[j], axis_send.at[j], axis_recv.at[j], sibling).wait_recv()
        total = total + axis_in[j]
    grad[c, yl, :, x] = total.reshape(2, unit // 2, half)

    g_begin()
    g_middle()
    g_late()
    g_end()
    g_finish()

    own = jnp.concatenate([grad[0, yl, c, x], grad[1, yl, c, x]], axis=1)
    for load in stat_loads:
        load.wait()
    moment = 0.99 * moment_ref[0] + 0.01 * own * own
    moment_out[0] = moment
    adam = own / (jnp.sqrt(moment) + 1e-08)
    adam_part = sum_all(adam * adam)

    for s in range(2):
        grad_hi[s], grad_lo[s] = split(grad[s].reshape(grad_hi.shape[1:]))

    def times_grad(value):
        rows = value.shape[0]
        high, low = split(value)
        both = jnp.concatenate([high, low], axis=0)
        out = []
        for s in range(2):
            wide = dot(both, grad_hi[s])
            out.append(wide[:rows] + (wide[rows:] + dot(high, grad_lo[s])))
        return jnp.concatenate(out, axis=1)

    mixed = times_grad(lroot_ref[0])
    mixed_hi, mixed_lo = split(mixed)
    wide = dot(jnp.concatenate([mixed_hi, mixed_lo], axis=0), rroot_hi[...])
    count = mixed.shape[0]
    precond = wide[:count] + (wide[count:] + dot(mixed_hi, rroot_lo[...]))
    precond_part = sum_all(precond * precond)

    lanes = norms.shape[2]
    rank = (yl * 2 + c) * NX + x
    norms[rank] = jnp.concatenate(
        [jnp.broadcast_to(adam_part, (1, lanes)), jnp.broadcast_to(precond_part, (1, lanes))], axis=0
    )
    for dx in range(NX):
        for dy in range(NL):
            for dc in range(2):
                if dx or dy or dc:
                    remote(
                        norms.at[rank], norms.at[rank], norm_send, norm_recv,
                        in_group((yl + dy) % NL, (c + dc) % 2, (x + dx) % NX),
                    ).start()

    own_hi, own_lo = split(own)
    both = jnp.concatenate([own_hi, own_lo], axis=0)
    outer = 0.95 * left_ref[0]
    for s in range(2):
        span = slice(s * half, (s + 1) * half)
        wide = dot_nt(both[:, span], grad_hi[s])
        outer = outer + (wide[:count] + (wide[count:] + dot_nt(own_hi[:, span], grad_lo[s])))
    left_out[0] = outer

    everyone = norms.at[pl.ds(0, norms.shape[0] - 1)]
    remote(everyone, everyone, norm_send, norm_recv, sibling).wait()
    sums = jnp.sum(norms[...], axis=0)
    scale = jnp.sqrt(sums[0:1, 0:1]) / (jnp.sqrt(sums[1:2, 0:1]) + 1e-06)
    updates[dp] = (scale * precond).astype(BF16)

    def update_copy(d, k, device):
        return remote(updates.at[d], updates.at[d], update_send.at[k], update_recv.at[d], device)

    across = z * 2 + (1 - yh)
    update_sent = [update_copy(dp, 0, at_yz((1 - yh) * NL + yl, z))]
    for k in range(1, NZ):
        update_sent.append(update_copy(dp, k, at_yz(y, (z + k) % NZ)))
    for copy in update_sent:
        copy.start()
    update_copy(across, 0, sibling).wait_recv()
    for k in range(1, NZ):
        copy = update_copy(across, NZ - 1 + k, at_yz(y, (z + k) % NZ))
        copy.start()
        update_sent.append(copy)
    pending.extend(update_sent)

    first = seq * (NX * count) + x * count
    lane = 128
    side = first // half
    tile = grad_hi.shape[1]
    strip = grad[side, :, :, :, :, pl.ds(pl.multiple_of((first % half) // lane * lane, lane), lane)]
    columns[...] = strip.reshape(tile, lane).T
    picked = columns[pl.ds(pl.multiple_of(first % lane, count), count)]
    right_out[0] = 0.95 * right_ref[0] + times_grad(picked)

    for k in range(1, NZ):
        for side_y in range(2):
            update_copy(((z + k) % NZ) * 2 + side_y, 0, sibling).wait_recv()
    for copy in pending:
        copy.wait_send()


def deliver(owner_ref, updates, left, right, moment, update_out, left_out, right_out, moment_out):
    for b in range(owner_ref.shape[0]):
        update_out[b] = updates[owner_ref[b]]
    left_out[...] = left[...]
    right_out[...] = right[...]
    moment_out[...] = moment[...]


def per_device(
    activations, d_logits, block_owner, left_stat, right_stat, second_moment, left_root, right_root
):
    tokens, width = activations.shape
    blocks = block_owner.shape[0]
    half = width // 2
    indices = jnp.arange(blocks, dtype=jnp.int32)
    owned = jnp.sum(jnp.where(block_owner[None, :] == indices[:, None], indices[None, :], 0), axis=1)
    rows = left_stat.shape[1]
    unit = 2 * rows
    vmem = pl.BlockSpec(memory_space=pltpu.VMEM)
    smem = pl.BlockSpec(memory_space=pltpu.SMEM)
    dma = pltpu.SemaphoreType.DMA
    stat = jax.ShapeDtypeStruct(left_stat.shape, F32)
    updates, left, right, moment = pl.pallas_call(
        kernel,
        out_shape=(jax.ShapeDtypeStruct((blocks, rows, width), BF16), stat, stat, stat),
        in_specs=[smem] + [pl.BlockSpec(memory_space=pltpu.HBM)] * 7,
        out_specs=(vmem,) * 4,
        scratch_shapes=[
            pltpu.VMEM((tokens, width), BF16),
            pltpu.VMEM(left_stat.shape, F32),
            pltpu.VMEM(left_stat.shape, F32),
            pltpu.VMEM(left_stat.shape, F32),
            pltpu.VMEM(left_stat.shape, F32),
            pltpu.VMEM((blocks, tokens, d_logits.shape[1] // blocks), BF16),
            pltpu.VMEM((blocks, tokens, d_logits.shape[1] // blocks), BF16),
            pltpu.VMEM((tokens, half), BF16),
            pltpu.VMEM((64, unit, half), F32),
            pltpu.VMEM((2, 4, 8, unit, half), F32),
            pltpu.VMEM((8, unit, half), F32),
            pltpu.VMEM((2, NL, 2, NX, rows, half), F32),
            pltpu.VMEM((NL, 2, NX, rows, width), F32),
            pltpu.VMEM((2, width, half), BF16),
            pltpu.VMEM((2, width, half), BF16),
            pltpu.VMEM((width, width), BF16),
            pltpu.VMEM((width, width), BF16),
            pltpu.VMEM((128, width), F32),
            pltpu.VMEM((32, 2, 128), F32),
            dma((7,)), dma((2,)), dma((2,)),
            dma((2, 4, PIECES)), dma((2, 4, PIECES)),
            dma((8,)), dma((8,)),
            dma((2, 24)), dma((2, 2, NL, NX)),
            dma, dma,
            dma((15,)), dma((16,)),
        ],
        compiler_params=pltpu.CompilerParams(
            collective_id=0, has_side_effects=True, vmem_limit_bytes=60 * 2**20
        ),
    )(owned, activations, d_logits, left_stat, right_stat, second_moment, left_root, right_root)
    return pl.pallas_call(
        deliver,
        out_shape=(jax.ShapeDtypeStruct(updates.shape, BF16), stat, stat, stat),
        in_specs=[smem] + [vmem] * 4,
        out_specs=(vmem,) * 4,
    )(block_owner, updates, left, right, moment)


def solution(mesh):
    shards = P("dp", ("seq", "tensor"), None)
    return jax.shard_map(
        per_device,
        mesh=mesh,
        in_specs=(P(("dp", "seq"), None), P(("dp", "seq"), "tensor"), P()) + (shards,) * 5,
        out_specs=(P(None, ("seq", "tensor"), None), shards, shards, shards),
        check_vma=False,
    )
```

```python
import jax
import jax.numpy as jnp
from jax import lax
from jax.experimental import pallas as pl
from jax.experimental.pallas import tpu as pltpu
from jax.sharding import PartitionSpec as P

F32 = jnp.float32
BF16 = jnp.bfloat16
MESH = pl.DeviceIdType.MESH

NZ = 8
NY = 8
NL = 4
NX = 4
PIECES = 4
FAR_FIRST = (4, 3, 5, 2, 6, 1, 7)
PIECE_ORDER = ((2, 3, 0, 1), (0, 1, 2, 3))


def split(value):
    high = value.astype(BF16)
    return high, (value - high.astype(F32)).astype(BF16)


def dot(a, b):
    return jnp.dot(a, b, preferred_element_type=F32)


def dot_nt(a, b):
    return lax.dot_general(a, b, (((1,), (1,)), ((), ())), preferred_element_type=F32)


def dot_tn(a, b):
    return lax.dot_general(a, b, (((0,), (0,)), ((), ())), preferred_element_type=F32)


def sum_all(value):
    return jnp.sum(jnp.sum(value, axis=0, keepdims=True), axis=1, keepdims=True)


def kernel(
    owned_ref, acts_hbm, logit_ref, left_hbm, right_hbm, moment_hbm, lroot_hbm, rroot_hbm,
    updates, left_out, right_out, moment_out,
    acts_ref, left_ref, right_ref, moments, lroots, logit_own, logit_other, acts_other, part, ring_in, axis_in, grad, rroot, grad_hi, grad_lo,
    rroot_hi, rroot_lo, columns, precond, adam_norms, norms,
    load_done, ex_send, ex_recv, ring_send, ring_recv, axis_send, axis_recv, gather_send, gather_recv,
    lroot_send, lroot_recv, adam_send, adam_recv, norm_send, norm_recv, update_send, update_recv,
):
    dp = lax.axis_index("dp")
    seq = lax.axis_index("seq")
    x = lax.axis_index("tensor")
    z, yh = dp // 2, dp % 2
    yl, c = seq // 2, seq % 2
    y = yh * NL + yl
    half = acts_ref.shape[1] // 2
    pending = []

    def at_yz(y_to, z_to):
        return (z_to * 2 + y_to // NL, (y_to % NL) * 2 + c, x)

    def in_group(yl_to, c_to, x_to):
        return (dp, yl_to * 2 + c_to, x_to)

    sibling = in_group(yl, 1 - c, x)
    i = (1 - c) * z + c * y
    me2 = (1 - c) * y + c * z

    def on_first(k):
        return at_yz((1 - c) * y + c * k, (1 - c) * k + c * z)

    def on_second(k):
        return at_yz((1 - c) * k + c * y, (1 - c) * z + c * k)

    ring_next = on_first((i + 1) % 8)
    ring_prev = on_first((i + 7) % 8)
    x_next, x_prev, x_far = (x + 1) % NX, (x + 3) % NX, (x + 2) % NX

    acts_load = pltpu.make_async_copy(acts_hbm, acts_ref, load_done.at[1])
    rroot_load = pltpu.make_async_copy(rroot_hbm.at[0], rroot.at[yl, c, x], load_done.at[2])
    stat_loads = [
        pltpu.make_async_copy(source, target, load_done.at[3 + k])
        for k, (source, target) in enumerate(
            ((left_hbm, left_ref), (right_hbm, right_ref), (moment_hbm.at[0], moments.at[c]))
        )
    ]
    lroot_load = pltpu.make_async_copy(lroot_hbm.at[0], lroots.at[c, x], load_done.at[6])
    rroot_load.start()
    acts_load.start()
    lroot_load.start()
    blocks = owned_ref.shape[0]
    band = logit_ref.shape[1] // blocks
    for b in range(blocks):
        pltpu.make_async_copy(logit_ref.at[:, pl.ds(b * band, band)], logit_own.at[b], load_done.at[0]).start()

    for load in stat_loads:
        load.start()

    barrier = pltpu.get_barrier_semaphore()

    def signal(device):
        pl.semaphore_signal(barrier, inc=1, device_id=device, device_id_type=MESH)

    partners = [at_yz((1 - yh) * NL + k, z) for k in range(NL)]
    partners += [at_yz(y, (z + k) % NZ) for k in FAR_FIRST]
    for k in (3, 2, 1, 0):
        yl_to = (yl, yl + 1 - 2 * (yl % 2), (yl + 2) % NL, NL - 1 - yl)[k]
        for dx in (2, 1, 3, 0):
            for dc in (1, 0):
                if dx or k or dc:
                    partners.append(in_group(yl_to, (c + dc) % 2, (x + dx) % NX))
    for device in partners:
        signal(device)
    pl.semaphore_wait(barrier, len(partners))

    def remote(src, dst, send, recv, device):
        return pltpu.make_async_remote_copy(
            src_ref=src, dst_ref=dst, send_sem=send, recv_sem=recv,
            device_id=device, device_id_type=MESH,
        )

    exchange = [
        remote(
            acts_hbm.at[:, pl.ds(pl.multiple_of((1 - c) * half, half), half)],
            acts_other, ex_send.at[0], ex_recv.at[0], sibling,
        )
    ]
    exchange[0].start()
    for b in range(blocks):
        strip = logit_ref.at[:, pl.ds(b * band, band)]
        remote(strip, logit_other.at[b], ex_send.at[1], ex_recv.at[1], sibling).start()
    exchange.append(remote(moment_hbm.at[0], moments.at[c], ex_send.at[2], ex_recv.at[2], sibling))
    exchange[1].start()
    exchange.append(remote(logit_other, logit_other, ex_send.at[1], ex_recv.at[1], sibling))

    def gather(which, slab, band_of):
        count = [0]

        def describe(place, k, core, q, column, device):
            return remote(
                place, place, gather_send.at[which, k], gather_recv.at[which, core, q, column], device
            )

        def arrive(q, column):
            describe(slab(q, c, column), 0, c, q, column, sibling).wait_recv()

        def launch(place, q, column, device):
            copy = describe(place, count[0], c, q, column, device)
            count[0] += 1
            copy.start()
            pending.append(copy)

        def push(q, column, device):
            launch(slab(q, c, column), q, column, device)

        def share(q):
            launch(band_of(q, c), q, 0, sibling)

        columns_to = [in_group(yl, c, column) for column in (x_far, x_next, x_prev)]

        def around(k):
            return (yl, yl + 1 - 2 * (yl % 2), (yl + 2) % NL, NL - 1 - yl)[k]

        def begin():
            for k in (3, 2, 1):
                push(yl, x, in_group(around(k), c, x))
            for device in columns_to:
                push(yl, x, device)

        def middle():
            for k in (1, 2, 3):
                arrive(around(k), x)
                for device in columns_to:
                    push(around(k), x, device)

        def late(k):
            for column in (x_next, x_prev, x_far):
                arrive(around(k), column)
            share(around(k))

        def finish():
            for q in range(NL):
                describe(band_of(q, 1 - c), 0, 1 - c, q, 0, sibling).wait_recv()

        return begin, middle, late, finish

    rroot_load.wait()
    r_begin, r_middle, r_late, r_finish = gather(
        0, lambda q, core, column: rroot.at[q, core, column], lambda q, core: rroot.at[q, core]
    )
    g_begin, g_middle, g_late, g_finish = gather(
        1, lambda q, core, column: grad.at[core, q, :, column], lambda q, core: grad.at[core, q]
    )
    r_begin()

    def lroot_copy(k, column, device):
        return remote(
            lroots.at[c, column], lroots.at[c, column], lroot_send.at[k], lroot_recv.at[0, column], device
        )

    def lroot_band(core):
        return remote(lroots.at[core], lroots.at[core], lroot_send.at[3], lroot_recv.at[1, 0], sibling)

    lroot_load.wait()
    for k, column in enumerate((x_far, x_next, x_prev)):
        copy = lroot_copy(k, x, in_group(yl, c, column))
        copy.start()
        pending.append(copy)

    unit = band // NL

    def place(d, q):
        row = (d % 2) * NL + q
        return (1 - c) * ((d // 2) * 8 + row) + c * (row * 8 + d // 2)

    def ordered(n):
        return (1 - c) * ((2 * (i + 4) + n) % 16) + c * (2 * (n % 8) + (yh + 1 + n // 8) % 2)

    def own_block(d, carry):
        rows = dot_tn(logit_own[owned_ref[d]], acts_own)
        for q in range(NL):
            part[place(d, q)] = rows[q * unit : (q + 1) * unit]
        return carry

    pltpu.make_async_copy(logit_own, logit_own, load_done.at[0]).wait()
    acts_load.wait()
    acts_own = acts_ref[:, pl.ds(pl.multiple_of(c * half, half), half)]
    lax.fori_loop(0, blocks, own_block, 0, unroll=4)
    for copy in exchange:
        copy.wait_recv()
    pending.extend(exchange)

    acts_rest = acts_other[...]

    def other_block(n, carry):
        d = ordered(n)
        rows = dot_tn(logit_other[owned_ref[d]], acts_rest)
        for q in range(NL):
            spot = place(d, q)
            part[spot] = part[spot] + rows[q * unit : (q + 1) * unit]
        return carry


    def chunk(way, step):
        return (i + 4 - step) % 8 if way == 0 else (i + 4 + step) % 8

    def ring(way, step, piece):
        return remote(
            part.at[pl.ds(chunk(way, step) * 8 + 2 * piece, 2)],
            ring_in.at[way, step, pl.ds(2 * piece, 2)],
            ring_send.at[way, step, piece], ring_recv.at[way, step, piece],
            (ring_next, ring_prev)[way],
        )

    def first_pieces(way):
        return (0, 1) if way == 0 else (2, 3)

    def ring_add(spot, way, step, piece):
        ring(way, step, piece).wait_recv()
        rows = pl.ds(spot * 8 + 2 * piece, 2)
        part[rows] = part[rows] + ring_in[way, step, pl.ds(2 * piece, 2)]

    def ring_send_off(way, step, piece):
        copy = ring(way, step, piece)
        copy.start()
        pending.append(copy)

    lax.fori_loop(0, blocks // 2, other_block, 0, unroll=4)
    for k in range(2):
        for way in range(2):
            ring_send_off(way, 0, first_pieces(way)[k])
    lax.fori_loop(blocks // 2, blocks, other_block, 0, unroll=4)
    for k in range(2):
        for way in range(2):
            ring_send_off(way, 1, PIECE_ORDER[way][k])
    r_middle()
    for step in range(1, 4):
        if step == 2:
            for column in (x_next, x_prev, x_far):
                lroot_copy(0, column, sibling).wait_recv()
            copy = lroot_band(c)
            copy.start()
            pending.append(copy)
            r_late(0)
            r_late(1)
        if step == 3:
            r_late(2)
            r_late(3)
        for k in range(PIECES):
            for way in range(2):
                piece = PIECE_ORDER[way][k]
                if step == 1 and k < 2:
                    continue
                ring_add(chunk(way, step), way, step - 1, piece)
                ring_send_off(way, step, piece)

    def axis_copy(j):
        return remote(
            part.at[i * 8 + j], axis_in.at[me2], axis_send.at[j], axis_recv.at[me2], on_second(j)
        )

    for k in range(PIECES):
        for way in range(2):
            ring_add(i, way, 3, PIECE_ORDER[way][k])
        for piece in {2: (0, 2), 3: (1, 3)}.get(k, ()):
            for j in (2 * piece, 2 * piece + 1):

                @pl.when(j != me2)
                def _():
                    axis_copy(j).start()

    for k in range(1, 8):
        pending.append(axis_copy((me2 + k) % 8))
    r_finish()
    lroot_band(1 - c).wait_recv()
    value = rroot[...].reshape(rroot_hi.shape)
    rroot_hi[...], rroot_lo[...] = split(value)

    total = part[i * 8 + me2]
    for k in range(1, 8):
        j = (me2 + k) % 8
        remote(part.at[i * 8 + j], axis_in.at[j], axis_send.at[j], axis_recv.at[j], sibling).wait_recv()
        total = total + axis_in[j]
    grad[c, yl, :, x] = total.reshape(2, unit // 2, half)

    g_begin()
    for load in stat_loads:
        load.wait()

    slab_grad = total.reshape(2, unit // 2, half)
    slab_moment = moments[:, :, pl.ds(pl.multiple_of(c * half, half), half)]
    slab_adam = slab_grad / (jnp.sqrt(0.99 * slab_moment + 0.01 * slab_grad * slab_grad) + 1e-08)
    lanes = norms.shape[2]
    rank = (yl * 2 + c) * NX + x
    adam_norms[rank] = jnp.broadcast_to(sum_all((slab_adam * slab_adam).reshape(unit, half)), (1, lanes))
    for k in range(NL):
        for dx in range(NX):
            for dc in range(2):
                if dx or k or dc:
                    remote(
                        adam_norms.at[rank], adam_norms.at[rank], adam_send, adam_recv,
                        in_group((yl + k) % NL, (c + dc) % 2, (x + dx) % NX),
                    ).start()

    count = lroots.shape[2]
    chip_rows = lroots.shape[0] * lroots.shape[1] * count
    lroot_hi, lroot_lo = split(lroots[...].reshape(chip_rows, lroots.shape[3]))
    lroot_both = jnp.concatenate([lroot_hi, lroot_lo], axis=0)
    g_middle()
    for k in range(NL):
        g_late(k)

    def precond_half(s):
        high, low = split(grad[s].reshape(grad_hi.shape[1:]))
        grad_hi[s] = high
        grad_lo[s] = low
        wide = dot(lroot_both, high)
        mixed = wide[:chip_rows] + (wide[chip_rows:] + dot(lroot_hi, low))
        mixed_hi, mixed_lo = split(mixed)
        span = pl.ds(pl.multiple_of(s * half, half), half)
        wide = dot(jnp.concatenate([mixed_hi, mixed_lo], axis=0), rroot_hi[span])
        return wide[:chip_rows] + (wide[chip_rows:] + dot(mixed_hi, rroot_lo[span]))

    precond[...] = precond_half(c).reshape(precond.shape)
    g_finish()
    chip_precond = precond[...].reshape(chip_rows, 2 * half) + precond_half(1 - c)
    precond[...] = chip_precond.reshape(precond.shape)

    norms[yl] = jnp.broadcast_to(sum_all(chip_precond * chip_precond), (1, lanes))
    for k in (3, 2, 1):
        yl_to = (yl, yl + 1 - 2 * (yl % 2), (yl + 2) % NL, NL - 1 - yl)[k]
        remote(norms.at[yl], norms.at[yl], norm_send, norm_recv, in_group(yl_to, c, x)).start()

    own = jnp.concatenate([grad[0, yl, c, x], grad[1, yl, c, x]], axis=1)
    moment_out[0] = 0.99 * moments[c] + 0.01 * own * own

    def times_grad(value):
        rows = value.shape[0]
        high, low = split(value)
        both = jnp.concatenate([high, low], axis=0)
        out = []
        for s in range(2):
            wide = dot(both, grad_hi[s])
            out.append(wide[:rows] + (wide[rows:] + dot(high, grad_lo[s])))
        return jnp.concatenate(out, axis=1)

    own_hi, own_lo = split(own)
    both = jnp.concatenate([own_hi, own_lo], axis=0)
    outer = 0.95 * left_ref[0]
    for s in range(2):
        span = slice(s * half, (s + 1) * half)
        wide = dot_nt(both[:, span], grad_hi[s])
        outer = outer + (wide[:count] + (wide[count:] + dot_nt(own_hi[:, span], grad_lo[s])))
    left_out[0] = outer

    everyone = adam_norms.at[pl.ds(0, adam_norms.shape[0] - 1)]
    remote(everyone, everyone, adam_send, adam_recv, sibling).wait()
    others = norms.at[pl.ds(0, NL - 1)]
    remote(others, others, norm_send, norm_recv, sibling).wait()
    adam_total = jnp.sum(adam_norms[...], axis=0)
    precond_total = jnp.sum(norms[...], axis=0)
    scale = jnp.sqrt(adam_total[:, 0:1]) / (jnp.sqrt(precond_total[:, 0:1]) + 1e-06)
    updates[dp] = (scale * precond[c * NX + x]).astype(BF16)

    def update_copy(d, k, device):
        return remote(updates.at[d], updates.at[d], update_send.at[k], update_recv.at[d], device)

    across = z * 2 + (1 - yh)
    update_sent = [update_copy(dp, 0, at_yz((1 - yh) * NL + yl, z))]
    for k in FAR_FIRST:
        update_sent.append(update_copy(dp, k, at_yz(y, (z + k) % NZ)))
    for copy in update_sent:
        copy.start()
    update_copy(across, 0, sibling).wait_recv()
    for k in FAR_FIRST:
        copy = update_copy(across, NZ - 1 + k, at_yz(y, (z + k) % NZ))
        copy.start()
        update_sent.append(copy)
    pending.extend(update_sent)

    first = seq * (NX * count) + x * count
    lane = 128
    side = first // half
    tile = grad_hi.shape[1]
    strip = grad[side, :, :, :, :, pl.ds(pl.multiple_of((first % half) // lane * lane, lane), lane)]
    columns[...] = strip.reshape(tile, lane).T
    picked = columns[pl.ds(pl.multiple_of(first % lane, count), count)]
    right_out[0] = 0.95 * right_ref[0] + times_grad(picked)

    for k in range(1, NZ):
        for side_y in range(2):
            update_copy(((z + k) % NZ) * 2 + side_y, 0, sibling).wait_recv()
    for copy in pending:
        copy.wait_send()


def deliver(owner_ref, updates, left, right, moment, update_out, left_out, right_out, moment_out):
    for b in range(owner_ref.shape[0]):
        update_out[b] = updates[owner_ref[b]]
    left_out[...] = left[...]
    right_out[...] = right[...]
    moment_out[...] = moment[...]


def per_device(
    activations, d_logits, block_owner, left_stat, right_stat, second_moment, left_root, right_root
):
    tokens, width = activations.shape
    blocks = block_owner.shape[0]
    half = width // 2
    indices = jnp.arange(blocks, dtype=jnp.int32)
    owned = jnp.sum(jnp.where(block_owner[None, :] == indices[:, None], indices[None, :], 0), axis=1)
    rows = left_stat.shape[1]
    unit = 2 * rows
    vmem = pl.BlockSpec(memory_space=pltpu.VMEM)
    smem = pl.BlockSpec(memory_space=pltpu.SMEM)
    dma = pltpu.SemaphoreType.DMA
    stat = jax.ShapeDtypeStruct(left_stat.shape, F32)
    updates, left, right, moment = pl.pallas_call(
        kernel,
        out_shape=(jax.ShapeDtypeStruct((blocks, rows, width), BF16), stat, stat, stat),
        in_specs=[smem] + [pl.BlockSpec(memory_space=pltpu.HBM)] * 7,
        out_specs=(vmem,) * 4,
        scratch_shapes=[
            pltpu.VMEM((tokens, width), BF16),
            pltpu.VMEM(left_stat.shape, F32),
            pltpu.VMEM(left_stat.shape, F32),
            pltpu.VMEM((2, rows, width), F32),
            pltpu.VMEM((2, NX, rows, width), F32),
            pltpu.VMEM((blocks, tokens, d_logits.shape[1] // blocks), BF16),
            pltpu.VMEM((blocks, tokens, d_logits.shape[1] // blocks), BF16),
            pltpu.VMEM((tokens, half), BF16),
            pltpu.VMEM((64, unit, half), F32),
            pltpu.VMEM((2, 4, 8, unit, half), F32),
            pltpu.VMEM((8, unit, half), F32),
            pltpu.VMEM((2, NL, 2, NX, rows, half), F32),
            pltpu.VMEM((NL, 2, NX, rows, width), F32),
            pltpu.VMEM((2, width, half), BF16),
            pltpu.VMEM((2, width, half), BF16),
            pltpu.VMEM((width, width), BF16),
            pltpu.VMEM((width, width), BF16),
            pltpu.VMEM((128, width), F32),
            pltpu.VMEM((2 * NX, rows, width), F32),
            pltpu.VMEM((32, 1, 128), F32),
            pltpu.VMEM((NL, 1, 128), F32),
            dma((7,)), dma((3,)), dma((3,)),
            dma((2, 4, PIECES)), dma((2, 4, PIECES)),
            dma((8,)), dma((8,)),
            dma((2, 24)), dma((2, 2, NL, NX)),
            dma((4,)), dma((2, NX)),
            dma, dma,
            dma, dma,
            dma((15,)), dma((16,)),
        ],
        compiler_params=pltpu.CompilerParams(
            collective_id=0, has_side_effects=True, vmem_limit_bytes=60 * 2**20
        ),
    )(owned, activations, d_logits, left_stat, right_stat, second_moment, left_root, right_root)
    return pl.pallas_call(
        deliver,
        out_shape=(jax.ShapeDtypeStruct(updates.shape, BF16), stat, stat, stat),
        in_specs=[smem] + [vmem] * 4,
        out_specs=(vmem,) * 4,
    )(block_owner, updates, left, right, moment)


def solution(mesh):
    shards = P("dp", ("seq", "tensor"), None)
    return jax.shard_map(
        per_device,
        mesh=mesh,
        in_specs=(P(("dp", "seq"), None), P(("dp", "seq"), "tensor"), P()) + (shards,) * 5,
        out_specs=(P(None, ("seq", "tensor"), None), shards, shards, shards),
        check_vma=False,
    )
```

```python
import jax
import jax.numpy as jnp
from jax import lax
from jax.experimental import pallas as pl
from jax.experimental.pallas import tpu as pltpu
from jax.sharding import PartitionSpec as P

F32 = jnp.float32
BF16 = jnp.bfloat16
MESH = pl.DeviceIdType.MESH

NZ = 8
NY = 8
NL = 4
NX = 4
PIECES = 4
FAR_FIRST = (4, 3, 5, 2, 6, 1, 7)
PIECE_ORDER = ((2, 3, 0, 1), (0, 1, 2, 3))


def split(value):
    high = value.astype(BF16)
    return high, (value - high.astype(F32)).astype(BF16)


def dot(a, b):
    return jnp.dot(a, b, preferred_element_type=F32)


def dot_nt(a, b):
    return lax.dot_general(a, b, (((1,), (1,)), ((), ())), preferred_element_type=F32)


def dot_tn(a, b):
    return lax.dot_general(a, b, (((0,), (0,)), ((), ())), preferred_element_type=F32)


def sum_all(value):
    return jnp.sum(jnp.sum(value, axis=0, keepdims=True), axis=1, keepdims=True)


def kernel(
    owner_ref, acts_hbm, logit_ref, left_hbm, right_hbm, moment_hbm, lroot_hbm, rroot_hbm,
    updates, left_out, right_out, moment_out,
    owned_ref, acts_ref, left_ref, right_ref, moments, lroots, logit_own, logit_other, acts_other, part, ring_in, axis_in, grad, rroot, grad_hi, grad_lo,
    rroot_hi, rroot_lo, columns, precond, adam_norms, norms,
    load_done, ex_send, ex_recv, ring_send, ring_recv, axis_send, axis_recv, gather_send, gather_recv,
    lroot_send, lroot_recv, adam_send, adam_recv, norm_send, norm_recv, update_send, update_recv,
):
    dp = lax.axis_index("dp")
    seq = lax.axis_index("seq")
    x = lax.axis_index("tensor")
    z, yh = dp // 2, dp % 2
    yl, c = seq // 2, seq % 2
    y = yh * NL + yl
    half = acts_ref.shape[1] // 2
    pending = []

    def at_yz(y_to, z_to):
        return (z_to * 2 + y_to // NL, (y_to % NL) * 2 + c, x)

    def in_group(yl_to, c_to, x_to):
        return (dp, yl_to * 2 + c_to, x_to)

    sibling = in_group(yl, 1 - c, x)
    i = (1 - c) * z + c * y
    me2 = (1 - c) * y + c * z

    def on_first(k):
        return at_yz((1 - c) * y + c * k, (1 - c) * k + c * z)

    def on_second(k):
        return at_yz((1 - c) * k + c * y, (1 - c) * z + c * k)

    ring_next = on_first((i + 1) % 8)
    ring_prev = on_first((i + 7) % 8)
    x_next, x_prev, x_far = (x + 1) % NX, (x + 3) % NX, (x + 2) % NX

    acts_load = pltpu.make_async_copy(acts_hbm, acts_ref, load_done.at[1])
    rroot_load = pltpu.make_async_copy(rroot_hbm.at[0], rroot.at[yl, c, x], load_done.at[2])
    stat_loads = [
        pltpu.make_async_copy(source, target, load_done.at[3 + k])
        for k, (source, target) in enumerate(
            ((left_hbm, left_ref), (right_hbm, right_ref), (moment_hbm.at[0], moments.at[c]))
        )
    ]
    lroot_load = pltpu.make_async_copy(lroot_hbm.at[0], lroots.at[c, x], load_done.at[6])
    rroot_load.start()
    acts_load.start()
    lroot_load.start()
    blocks = owner_ref.shape[0]
    band = logit_ref.shape[1] // blocks
    for b in range(blocks):
        pltpu.make_async_copy(logit_ref.at[:, pl.ds(b * band, band)], logit_own.at[b], load_done.at[0]).start()

    for load in stat_loads:
        load.start()

    barrier = pltpu.get_barrier_semaphore()

    def signal(device):
        pl.semaphore_signal(barrier, inc=1, device_id=device, device_id_type=MESH)

    partners = [at_yz((1 - yh) * NL + k, z) for k in range(NL)]
    partners += [at_yz(y, (z + k) % NZ) for k in FAR_FIRST]
    partners += [in_group((yl + k) % NL, c, x) for k in range(1, NL)]
    partners += [in_group(yl, c, column) for column in (x_far, x_next, x_prev)] + [sibling]
    for device in partners:
        signal(device)
    pl.semaphore_wait(barrier, len(partners))

    def remote(src, dst, send, recv, device):
        return pltpu.make_async_remote_copy(
            src_ref=src, dst_ref=dst, send_sem=send, recv_sem=recv,
            device_id=device, device_id_type=MESH,
        )

    exchange = [
        remote(
            acts_hbm.at[:, pl.ds(pl.multiple_of((1 - c) * half, half), half)],
            acts_other, ex_send.at[0], ex_recv.at[0], sibling,
        )
    ]
    exchange[0].start()
    for b in range(blocks):
        strip = logit_ref.at[:, pl.ds(b * band, band)]
        remote(strip, logit_other.at[b], ex_send.at[1], ex_recv.at[1], sibling).start()
    exchange.append(remote(moment_hbm.at[0], moments.at[c], ex_send.at[2], ex_recv.at[2], sibling))
    exchange[1].start()
    exchange.append(remote(logit_other, logit_other, ex_send.at[1], ex_recv.at[1], sibling))

    def gather(which, slab, band_of):
        count = [0]

        def describe(place, k, core, q, column, device):
            return remote(
                place, place, gather_send.at[which, k], gather_recv.at[which, core, q, column], device
            )

        def arrive(q, column):
            describe(slab(q, c, column), 0, c, q, column, sibling).wait_recv()

        def launch(place, q, column, device):
            copy = describe(place, count[0], c, q, column, device)
            count[0] += 1
            copy.start()
            pending.append(copy)

        def push(q, column, device):
            launch(slab(q, c, column), q, column, device)

        def share(q):
            launch(band_of(q, c), q, 0, sibling)

        columns_to = [in_group(yl, c, column) for column in (x_far, x_next, x_prev)]

        def around(k):
            return (yl, yl + 1 - 2 * (yl % 2), (yl + 2) % NL, NL - 1 - yl)[k]

        def begin():
            for k in (3, 2, 1):
                push(yl, x, in_group(around(k), c, x))
            for device in columns_to:
                push(yl, x, device)

        def middle():
            for k in (1, 2, 3):
                arrive(around(k), x)
                for device in columns_to:
                    push(around(k), x, device)

        def late(k):
            for column in (x_next, x_prev, x_far):
                arrive(around(k), column)
            share(around(k))

        def finish():
            for q in range(NL):
                describe(band_of(q, 1 - c), 0, 1 - c, q, 0, sibling).wait_recv()

        return begin, middle, late, finish

    rroot_load.wait()
    r_begin, r_middle, r_late, r_finish = gather(
        0, lambda q, core, column: rroot.at[q, core, column], lambda q, core: rroot.at[q, core]
    )
    g_begin, g_middle, g_late, g_finish = gather(
        1, lambda q, core, column: grad.at[core, q, :, column], lambda q, core: grad.at[core, q]
    )
    r_begin()

    def lroot_copy(k, column, device):
        return remote(
            lroots.at[c, column], lroots.at[c, column], lroot_send.at[k], lroot_recv.at[0, column], device
        )

    def lroot_band(core):
        return remote(lroots.at[core], lroots.at[core], lroot_send.at[3], lroot_recv.at[1, 0], sibling)

    lroot_load.wait()
    for k, column in enumerate((x_far, x_next, x_prev)):
        copy = lroot_copy(k, x, in_group(yl, c, column))
        copy.start()
        pending.append(copy)

    unit = band // NL

    def place(d, q):
        row = (d % 2) * NL + q
        return (1 - c) * ((d // 2) * 8 + row) + c * (row * 8 + d // 2)

    def ordered(n):
        return (1 - c) * ((2 * (i + 4) + n) % 16) + c * (2 * (n % 8) + (yh + 1 + n // 8) % 2)

    def own_block(d, carry):
        b = jnp.int32(0)
        for k in range(1, blocks):
            apart = owner_ref[k] - d
            b = b + k * lax.shift_right_logical(blocks * blocks - apart * apart, jnp.int32(8))
        b = lax.rem(b, jnp.int32(blocks))
        owned_ref[d] = b
        rows = dot_tn(logit_own[b], acts_own)
        for q in range(NL):
            part[place(d, q)] = rows[q * unit : (q + 1) * unit]
        return carry

    pltpu.make_async_copy(logit_own, logit_own, load_done.at[0]).wait()
    acts_load.wait()
    acts_own = acts_ref[:, pl.ds(pl.multiple_of(c * half, half), half)]
    lax.fori_loop(0, blocks, own_block, 0, unroll=4)
    for copy in exchange:
        copy.wait_recv()
    pending.extend(exchange)

    acts_rest = acts_other[...]

    def other_block(n, carry):
        d = ordered(n)
        rows = dot_tn(logit_other[owned_ref[d]], acts_rest)
        for q in range(NL):
            spot = place(d, q)
            part[spot] = part[spot] + rows[q * unit : (q + 1) * unit]
        return carry


    def chunk(way, step):
        return (i + 4 - step) % 8 if way == 0 else (i + 4 + step) % 8

    def ring(way, step, piece):
        return remote(
            part.at[pl.ds(chunk(way, step) * 8 + 2 * piece, 2)],
            ring_in.at[way, step, pl.ds(2 * piece, 2)],
            ring_send.at[way, step, piece], ring_recv.at[way, step, piece],
            (ring_next, ring_prev)[way],
        )

    def first_pieces(way):
        return (0, 1) if way == 0 else (2, 3)

    def ring_add(spot, way, step, piece):
        ring(way, step, piece).wait_recv()
        rows = pl.ds(spot * 8 + 2 * piece, 2)
        part[rows] = part[rows] + ring_in[way, step, pl.ds(2 * piece, 2)]

    def ring_send_off(way, step, piece):
        copy = ring(way, step, piece)
        copy.start()
        pending.append(copy)

    lax.fori_loop(0, blocks // 2, other_block, 0, unroll=4)
    for k in range(2):
        for way in range(2):
            ring_send_off(way, 0, first_pieces(way)[k])
    lax.fori_loop(blocks // 2, blocks, other_block, 0, unroll=4)
    for k in range(2):
        for way in range(2):
            ring_send_off(way, 1, PIECE_ORDER[way][k])
    r_middle()
    for step in range(1, 4):
        if step == 2:
            for column in (x_next, x_prev, x_far):
                lroot_copy(0, column, sibling).wait_recv()
            copy = lroot_band(c)
            copy.start()
            pending.append(copy)
            r_late(0)
            r_late(1)
        if step == 3:
            r_late(2)
            r_late(3)
        for k in range(PIECES):
            for way in range(2):
                piece = PIECE_ORDER[way][k]
                if step == 1 and k < 2:
                    continue
                ring_add(chunk(way, step), way, step - 1, piece)
                ring_send_off(way, step, piece)

    def axis_copy(j):
        return remote(
            part.at[i * 8 + j], axis_in.at[me2], axis_send.at[j], axis_recv.at[me2], on_second(j)
        )

    for k in range(PIECES):
        for way in range(2):
            ring_add(i, way, 3, PIECE_ORDER[way][k])
        for piece in {2: (0, 2), 3: (1, 3)}.get(k, ()):
            for j in (2 * piece, 2 * piece + 1):

                @pl.when(j != me2)
                def _():
                    axis_copy(j).start()

    for k in range(1, 8):
        pending.append(axis_copy((me2 + k) % 8))
    r_finish()
    lroot_band(1 - c).wait_recv()
    value = rroot[...].reshape(rroot_hi.shape)
    rroot_hi[...], rroot_lo[...] = split(value)

    total = part[i * 8 + me2]
    for k in range(1, 8):
        j = (me2 + k) % 8
        remote(part.at[i * 8 + j], axis_in.at[j], axis_send.at[j], axis_recv.at[j], sibling).wait_recv()
        total = total + axis_in[j]
    grad[c, yl, :, x] = total.reshape(2, unit // 2, half)

    g_begin()
    for load in stat_loads:
        load.wait()

    slab_grad = total.reshape(2, unit // 2, half)
    slab_moment = moments[:, :, pl.ds(pl.multiple_of(c * half, half), half)]
    slab_adam = slab_grad / (jnp.sqrt(0.99 * slab_moment + 0.01 * slab_grad * slab_grad) + 1e-08)
    lanes = norms.shape[2]

    def adam_copy(level, place, device):
        spot = adam_norms.at[level, place]
        return remote(spot, spot, adam_send.at[level], adam_recv.at[level], device)

    def adam_sum(level, others):
        several = adam_norms.at[level, pl.ds(0, others)]
        remote(several, several, adam_send.at[level], adam_recv.at[level], sibling).wait()
        return jnp.sum(adam_norms[level, 0 : others + 1], axis=0)

    adam_norms[0, c] = jnp.broadcast_to(sum_all((slab_adam * slab_adam).reshape(unit, half)), (1, lanes))
    adam_copy(0, c, sibling).start()
    count = lroots.shape[2]
    chip_rows = lroots.shape[0] * lroots.shape[1] * count
    lroot_hi, lroot_lo = split(lroots[...].reshape(chip_rows, lroots.shape[3]))
    lroot_both = jnp.concatenate([lroot_hi, lroot_lo], axis=0)
    adam_norms[1, x] = adam_sum(0, 1)
    for column in (x_far, x_next, x_prev):
        adam_copy(1, x, in_group(yl, c, column)).start()
    g_middle()
    adam_norms[2, yl] = adam_sum(1, NX - 1)
    for k in range(1, NL):
        adam_copy(2, yl, in_group((yl + k) % NL, c, x)).start()
    for k in range(NL):
        g_late(k)
    adam_total = adam_sum(2, NL - 1)

    def precond_half(s):
        high, low = split(grad[s].reshape(grad_hi.shape[1:]))
        grad_hi[s] = high
        grad_lo[s] = low
        wide = dot(lroot_both, high)
        mixed = wide[:chip_rows] + (wide[chip_rows:] + dot(lroot_hi, low))
        mixed_hi, mixed_lo = split(mixed)
        span = pl.ds(pl.multiple_of(s * half, half), half)
        wide = dot(jnp.concatenate([mixed_hi, mixed_lo], axis=0), rroot_hi[span])
        return wide[:chip_rows] + (wide[chip_rows:] + dot(mixed_hi, rroot_lo[span]))

    precond[...] = precond_half(c).reshape(precond.shape)
    g_finish()
    chip_precond = precond[...].reshape(chip_rows, 2 * half) + precond_half(1 - c)
    precond[...] = chip_precond.reshape(precond.shape)

    norms[yl] = jnp.broadcast_to(sum_all(chip_precond * chip_precond), (1, lanes))
    for k in (3, 2, 1):
        yl_to = (yl, yl + 1 - 2 * (yl % 2), (yl + 2) % NL, NL - 1 - yl)[k]
        remote(norms.at[yl], norms.at[yl], norm_send, norm_recv, in_group(yl_to, c, x)).start()

    own = jnp.concatenate([grad[0, yl, c, x], grad[1, yl, c, x]], axis=1)
    moment_out[0] = 0.99 * moments[c] + 0.01 * own * own

    def times_grad(value):
        rows = value.shape[0]
        high, low = split(value)
        both = jnp.concatenate([high, low], axis=0)
        out = []
        for s in range(2):
            wide = dot(both, grad_hi[s])
            out.append(wide[:rows] + (wide[rows:] + dot(high, grad_lo[s])))
        return jnp.concatenate(out, axis=1)

    own_hi, own_lo = split(own)
    both = jnp.concatenate([own_hi, own_lo], axis=0)
    outer = 0.95 * left_ref[0]
    for s in range(2):
        span = slice(s * half, (s + 1) * half)
        wide = dot_nt(both[:, span], grad_hi[s])
        outer = outer + (wide[:count] + (wide[count:] + dot_nt(own_hi[:, span], grad_lo[s])))
    left_out[0] = outer

    others = norms.at[pl.ds(0, NL - 1)]
    remote(others, others, norm_send, norm_recv, sibling).wait()
    precond_total = jnp.sum(norms[...], axis=0)
    scale = jnp.sqrt(adam_total[:, 0:1]) / (jnp.sqrt(precond_total[:, 0:1]) + 1e-06)
    updates[dp] = (scale * precond[c * NX + x]).astype(BF16)

    def update_copy(d, k, device):
        return remote(updates.at[d], updates.at[d], update_send.at[k], update_recv.at[d], device)

    across = z * 2 + (1 - yh)
    update_sent = [update_copy(dp, 0, at_yz((1 - yh) * NL + yl, z))]
    for k in FAR_FIRST:
        update_sent.append(update_copy(dp, k, at_yz(y, (z + k) % NZ)))
    for copy in update_sent:
        copy.start()
    update_copy(across, 0, sibling).wait_recv()
    for k in FAR_FIRST:
        copy = update_copy(across, NZ - 1 + k, at_yz(y, (z + k) % NZ))
        copy.start()
        update_sent.append(copy)
    pending.extend(update_sent)

    first = seq * (NX * count) + x * count
    lane = 128
    side = first // half
    tile = grad_hi.shape[1]
    strip = grad[side, :, :, :, :, pl.ds(pl.multiple_of((first % half) // lane * lane, lane), lane)]
    columns[...] = strip.reshape(tile, lane).T
    picked = columns[pl.ds(pl.multiple_of(first % lane, count), count)]
    right_out[0] = 0.95 * right_ref[0] + times_grad(picked)

    for k in range(1, NZ):
        for side_y in range(2):
            update_copy(((z + k) % NZ) * 2 + side_y, 0, sibling).wait_recv()
    for copy in pending:
        copy.wait_send()


def deliver(owner_ref, updates, left, right, moment, update_out, left_out, right_out, moment_out):
    for b in range(owner_ref.shape[0]):
        update_out[b] = updates[owner_ref[b]]
    left_out[...] = left[...]
    right_out[...] = right[...]
    moment_out[...] = moment[...]


def per_device(
    activations, d_logits, block_owner, left_stat, right_stat, second_moment, left_root, right_root
):
    tokens, width = activations.shape
    blocks = block_owner.shape[0]
    half = width // 2
    rows = left_stat.shape[1]
    unit = 2 * rows
    vmem = pl.BlockSpec(memory_space=pltpu.VMEM)
    smem = pl.BlockSpec(memory_space=pltpu.SMEM)
    dma = pltpu.SemaphoreType.DMA
    stat = jax.ShapeDtypeStruct(left_stat.shape, F32)
    updates, left, right, moment = pl.pallas_call(
        kernel,
        out_shape=(jax.ShapeDtypeStruct((blocks, rows, width), BF16), stat, stat, stat),
        in_specs=[smem] + [pl.BlockSpec(memory_space=pltpu.HBM)] * 7,
        out_specs=(vmem,) * 4,
        scratch_shapes=[
            pltpu.SMEM((blocks,), jnp.int32),
            pltpu.VMEM((tokens, width), BF16),
            pltpu.VMEM(left_stat.shape, F32),
            pltpu.VMEM(left_stat.shape, F32),
            pltpu.VMEM((2, rows, width), F32),
            pltpu.VMEM((2, NX, rows, width), F32),
            pltpu.VMEM((blocks, tokens, d_logits.shape[1] // blocks), BF16),
            pltpu.VMEM((blocks, tokens, d_logits.shape[1] // blocks), BF16),
            pltpu.VMEM((tokens, half), BF16),
            pltpu.VMEM((64, unit, half), F32),
            pltpu.VMEM((2, 4, 8, unit, half), F32),
            pltpu.VMEM((8, unit, half), F32),
            pltpu.VMEM((2, NL, 2, NX, rows, half), F32),
            pltpu.VMEM((NL, 2, NX, rows, width), F32),
            pltpu.VMEM((2, width, half), BF16),
            pltpu.VMEM((2, width, half), BF16),
            pltpu.VMEM((width, width), BF16),
            pltpu.VMEM((width, width), BF16),
            pltpu.VMEM((128, width), F32),
            pltpu.VMEM((2 * NX, rows, width), F32),
            pltpu.VMEM((3, NX, 1, 128), F32),
            pltpu.VMEM((NL, 1, 128), F32),
            dma((7,)), dma((3,)), dma((3,)),
            dma((2, 4, PIECES)), dma((2, 4, PIECES)),
            dma((8,)), dma((8,)),
            dma((2, 24)), dma((2, 2, NL, NX)),
            dma((4,)), dma((2, NX)),
            dma((3,)), dma((3,)),
            dma, dma,
            dma((15,)), dma((16,)),
        ],
        compiler_params=pltpu.CompilerParams(
            collective_id=0, has_side_effects=True, vmem_limit_bytes=60 * 2**20
        ),
    )(block_owner, activations, d_logits, left_stat, right_stat, second_moment, left_root, right_root)
    return pl.pallas_call(
        deliver,
        out_shape=(jax.ShapeDtypeStruct(updates.shape, BF16), stat, stat, stat),
        in_specs=[smem] + [vmem] * 4,
        out_specs=(vmem,) * 4,
    )(block_owner, updates, left, right, moment)


def solution(mesh):
    shards = P("dp", ("seq", "tensor"), None)
    return jax.shard_map(
        per_device,
        mesh=mesh,
        in_specs=(P(("dp", "seq"), None), P(("dp", "seq"), "tensor"), P()) + (shards,) * 5,
        out_specs=(P(None, ("seq", "tensor"), None), shards, shards, shards),
        check_vma=False,
    )
```

```python
import jax
import jax.numpy as jnp
from jax import lax
from jax.experimental import pallas as pl
from jax.experimental.pallas import tpu as pltpu
from jax.sharding import PartitionSpec as P

F32 = jnp.float32
BF16 = jnp.bfloat16
MESH = pl.DeviceIdType.MESH

NZ = 8
NY = 8
NL = 4
NX = 4
PIECES = 4
FAR_FIRST = (4, 3, 5, 2, 6, 1, 7)
PIECE_ORDER = ((2, 3, 0, 1), (0, 1, 2, 3))


def split(value):
    high = value.astype(BF16)
    return high, (value - high.astype(F32)).astype(BF16)


def dot(a, b):
    return jnp.dot(a, b, preferred_element_type=F32)


def dot_nt(a, b):
    return lax.dot_general(a, b, (((1,), (1,)), ((), ())), preferred_element_type=F32)


def dot_tn(a, b):
    return lax.dot_general(a, b, (((0,), (0,)), ((), ())), preferred_element_type=F32)


def sum_all(value):
    return jnp.sum(jnp.sum(value, axis=0, keepdims=True), axis=1, keepdims=True)


def kernel(
    owner_ref, acts_hbm, logit_ref, left_hbm, right_hbm, moment_hbm, lroot_hbm, rroot_hbm,
    updates, left_out, right_out, moment_out,
    owned_ref, acts_ref, left_ref, right_ref, moments, lroots, logit_own, logit_other, acts_other, part, ring_in, axis_in, grad, rroot, grad_hi, grad_lo,
    rroot_hi, rroot_lo, columns, precond, adam_norms, norms,
    load_done, ex_send, ex_recv, ring_send, ring_recv, axis_send, axis_recv, gather_send, gather_recv,
    lroot_send, lroot_recv, adam_send, adam_recv, norm_send, norm_recv, update_send, update_recv,
):
    dp = lax.axis_index("dp")
    seq = lax.axis_index("seq")
    x = lax.axis_index("tensor")
    z, yh = dp // 2, dp % 2
    yl, c = seq // 2, seq % 2
    y = yh * NL + yl
    half = acts_ref.shape[1] // 2
    pending = []

    def at_yz(y_to, z_to):
        return (z_to * 2 + y_to // NL, (y_to % NL) * 2 + c, x)

    def in_group(yl_to, c_to, x_to):
        return (dp, yl_to * 2 + c_to, x_to)

    sibling = in_group(yl, 1 - c, x)
    i = (1 - c) * z + c * y
    me2 = (1 - c) * y + c * z

    def on_first(k):
        return at_yz((1 - c) * y + c * k, (1 - c) * k + c * z)

    def on_second(k):
        return at_yz((1 - c) * k + c * y, (1 - c) * z + c * k)

    ring_next = on_first((i + 1) % 8)
    ring_prev = on_first((i + 7) % 8)
    x_next, x_prev, x_far = (x + 1) % NX, (x + 3) % NX, (x + 2) % NX

    acts_load = pltpu.make_async_copy(acts_hbm, acts_ref, load_done.at[1])
    rroot_load = pltpu.make_async_copy(rroot_hbm.at[0], rroot.at[yl, c, x], load_done.at[2])
    stat_loads = [
        pltpu.make_async_copy(source, target, load_done.at[3 + k])
        for k, (source, target) in enumerate(
            ((left_hbm, left_ref), (right_hbm, right_ref), (moment_hbm.at[0], moments.at[c]))
        )
    ]
    lroot_load = pltpu.make_async_copy(lroot_hbm.at[0], lroots.at[c, x], load_done.at[6])
    rroot_load.start()
    acts_load.start()
    lroot_load.start()
    blocks = owner_ref.shape[0]
    band = logit_ref.shape[1] // blocks
    for b in range(blocks):
        pltpu.make_async_copy(logit_ref.at[:, pl.ds(b * band, band)], logit_own.at[b], load_done.at[0]).start()

    for load in stat_loads:
        load.start()

    barrier = pltpu.get_barrier_semaphore()

    def signal(device):
        pl.semaphore_signal(barrier, inc=1, device_id=device, device_id_type=MESH)

    partners = [at_yz((1 - yh) * NL + k, z) for k in range(NL)]
    partners += [at_yz(y, (z + k) % NZ) for k in FAR_FIRST]
    partners += [in_group((yl + k) % NL, c, x) for k in range(1, NL)]
    partners += [in_group(yl, c, column) for column in (x_far, x_next, x_prev)] + [sibling]
    for device in partners:
        signal(device)
    pl.semaphore_wait(barrier, len(partners))

    def remote(src, dst, send, recv, device):
        return pltpu.make_async_remote_copy(
            src_ref=src, dst_ref=dst, send_sem=send, recv_sem=recv,
            device_id=device, device_id_type=MESH,
        )

    exchange = [
        remote(
            acts_hbm.at[:, pl.ds(pl.multiple_of((1 - c) * half, half), half)],
            acts_other, ex_send.at[0], ex_recv.at[0], sibling,
        )
    ]
    exchange[0].start()
    for b in range(blocks):
        strip = logit_ref.at[:, pl.ds(b * band, band)]
        remote(strip, logit_other.at[b], ex_send.at[1], ex_recv.at[1], sibling).start()
    exchange.append(remote(moment_hbm.at[0], moments.at[c], ex_send.at[2], ex_recv.at[2], sibling))
    exchange[1].start()
    exchange.append(remote(logit_other, logit_other, ex_send.at[1], ex_recv.at[1], sibling))

    def gather(which, slab, band_of):
        count = [0]

        def describe(place, k, core, q, column, device):
            return remote(
                place, place, gather_send.at[which, k], gather_recv.at[which, core, q, column], device
            )

        def arrive(q, column):
            describe(slab(q, c, column), 0, c, q, column, sibling).wait_recv()

        def launch(place, q, column, device):
            copy = describe(place, count[0], c, q, column, device)
            count[0] += 1
            copy.start()
            pending.append(copy)

        def push(q, column, device):
            launch(slab(q, c, column), q, column, device)

        def share(q):
            launch(band_of(q, c), q, 0, sibling)

        columns_to = [in_group(yl, c, column) for column in (x_far, x_next, x_prev)]

        def around(k):
            return (yl, yl + 1 - 2 * (yl % 2), (yl + 2) % NL, NL - 1 - yl)[k]

        def begin():
            for k in (3, 2, 1):
                push(yl, x, in_group(around(k), c, x))
            for device in columns_to:
                push(yl, x, device)

        def middle():
            for k in (1, 2, 3):
                arrive(around(k), x)
                for device in columns_to:
                    push(around(k), x, device)

        def late(k):
            for column in (x_next, x_prev, x_far):
                arrive(around(k), column)
            share(around(k))

        def finish():
            for q in range(NL):
                describe(band_of(q, 1 - c), 0, 1 - c, q, 0, sibling).wait_recv()

        return begin, middle, late, finish

    rroot_load.wait()
    r_begin, r_middle, r_late, r_finish = gather(
        0, lambda q, core, column: rroot.at[q, core, column], lambda q, core: rroot.at[q, core]
    )
    g_begin, g_middle, g_late, g_finish = gather(
        1, lambda q, core, column: grad.at[core, q, :, column], lambda q, core: grad.at[core, q]
    )

    def lroot_copy(k, column, device):
        return remote(
            lroots.at[c, column], lroots.at[c, column], lroot_send.at[k], lroot_recv.at[0, column], device
        )

    def lroot_band(core):
        return remote(lroots.at[core], lroots.at[core], lroot_send.at[3], lroot_recv.at[1, 0], sibling)

    unit = band // NL

    def place(d, q):
        row = (d % 2) * NL + q
        return (1 - c) * ((d // 2) * 8 + row) + c * (row * 8 + d // 2)

    def ordered(n):
        return (1 - c) * ((2 * (i + 4) + n) % 16) + c * (2 * (n % 8) + (yh + 1 + n // 8) % 2)

    def own_block(d, carry):
        b = jnp.int32(0)
        for k in range(1, blocks):
            apart = owner_ref[k] - d
            b = b + k * lax.shift_right_logical(blocks * blocks - apart * apart, jnp.int32(8))
        b = lax.rem(b, jnp.int32(blocks))
        owned_ref[d] = b
        rows = dot_tn(logit_own[b], acts_own)
        for q in range(NL):
            part[place(d, q)] = rows[q * unit : (q + 1) * unit]
        return carry

    pltpu.make_async_copy(logit_own, logit_own, load_done.at[0]).wait()
    acts_load.wait()
    acts_own = acts_ref[:, pl.ds(pl.multiple_of(c * half, half), half)]
    lax.fori_loop(0, blocks, own_block, 0, unroll=4)
    r_begin()
    lroot_load.wait()
    for k, column in enumerate((x_far, x_next, x_prev)):
        copy = lroot_copy(k, x, in_group(yl, c, column))
        copy.start()
        pending.append(copy)

    for copy in exchange:
        copy.wait_recv()
    pending.extend(exchange)

    acts_rest = acts_other[...]

    def other_block(n, carry):
        d = ordered(n)
        rows = dot_tn(logit_other[owned_ref[d]], acts_rest)
        for q in range(NL):
            spot = place(d, q)
            part[spot] = part[spot] + rows[q * unit : (q + 1) * unit]
        return carry


    def chunk(way, step):
        return (i + 4 - step) % 8 if way == 0 else (i + 4 + step) % 8

    def ring(way, step, piece):
        return remote(
            part.at[pl.ds(chunk(way, step) * 8 + 2 * piece, 2)],
            ring_in.at[way, step, pl.ds(2 * piece, 2)],
            ring_send.at[way, step, piece], ring_recv.at[way, step, piece],
            (ring_next, ring_prev)[way],
        )

    def first_pieces(way):
        return (0, 1) if way == 0 else (2, 3)

    def ring_add(spot, way, step, piece):
        ring(way, step, piece).wait_recv()
        rows = pl.ds(spot * 8 + 2 * piece, 2)
        part[rows] = part[rows] + ring_in[way, step, pl.ds(2 * piece, 2)]

    def ring_send_off(way, step, piece):
        copy = ring(way, step, piece)
        copy.start()
        pending.append(copy)

    lax.fori_loop(0, blocks // 2, other_block, 0, unroll=4)
    for k in range(2):
        for way in range(2):
            ring_send_off(way, 0, first_pieces(way)[k])
    lax.fori_loop(blocks // 2, blocks, other_block, 0, unroll=4)
    for k in range(2):
        for way in range(2):
            ring_send_off(way, 1, PIECE_ORDER[way][k])
    r_middle()
    for step in range(1, 4):
        if step == 2:
            pass
        for k in range(PIECES):
            for way in range(2):
                piece = PIECE_ORDER[way][k]
                if step == 1 and k < 2:
                    continue
                ring_add(chunk(way, step), way, step - 1, piece)
                ring_send_off(way, step, piece)

    def axis_copy(j):
        return remote(
            part.at[i * 8 + j], axis_in.at[me2], axis_send.at[j], axis_recv.at[me2], on_second(j)
        )

    for k in range(PIECES):
        for way in range(2):
            ring_add(i, way, 3, PIECE_ORDER[way][k])
        for piece in {2: (0, 2), 3: (1, 3)}.get(k, ()):
            for j in (2 * piece, 2 * piece + 1):

                @pl.when(j != me2)
                def _():
                    axis_copy(j).start()

    for k in range(1, 8):
        pending.append(axis_copy((me2 + k) % 8))
    for k in range(NL):
        r_late(k)
    for column in (x_next, x_prev, x_far):
        lroot_copy(0, column, sibling).wait_recv()
    copy = lroot_band(c)
    copy.start()
    pending.append(copy)
    r_finish()
    lroot_band(1 - c).wait_recv()
    value = rroot[...].reshape(rroot_hi.shape)
    rroot_hi[...], rroot_lo[...] = split(value)

    total = part[i * 8 + me2]
    for k in range(1, 8):
        j = (me2 + k) % 8
        remote(part.at[i * 8 + j], axis_in.at[j], axis_send.at[j], axis_recv.at[j], sibling).wait_recv()
        total = total + axis_in[j]
    grad[c, yl, :, x] = total.reshape(2, unit // 2, half)

    g_begin()
    for load in stat_loads:
        load.wait()

    slab_grad = total.reshape(2, unit // 2, half)
    slab_moment = moments[:, :, pl.ds(pl.multiple_of(c * half, half), half)]
    slab_adam = slab_grad / (jnp.sqrt(0.99 * slab_moment + 0.01 * slab_grad * slab_grad) + 1e-08)
    lanes = norms.shape[2]

    def adam_copy(level, place, device):
        spot = adam_norms.at[level, place]
        return remote(spot, spot, adam_send.at[level], adam_recv.at[level], device)

    def adam_sum(level, others):
        several = adam_norms.at[level, pl.ds(0, others)]
        remote(several, several, adam_send.at[level], adam_recv.at[level], sibling).wait()
        return jnp.sum(adam_norms[level, 0 : others + 1], axis=0)

    adam_norms[0, c] = jnp.broadcast_to(sum_all((slab_adam * slab_adam).reshape(unit, half)), (1, lanes))
    adam_copy(0, c, sibling).start()
    count = lroots.shape[2]
    chip_rows = lroots.shape[0] * lroots.shape[1] * count
    lroot_hi, lroot_lo = split(lroots[...].reshape(chip_rows, lroots.shape[3]))
    lroot_both = jnp.concatenate([lroot_hi, lroot_lo], axis=0)
    adam_norms[1, x] = adam_sum(0, 1)
    for column in (x_far, x_next, x_prev):
        adam_copy(1, x, in_group(yl, c, column)).start()
    g_middle()
    adam_norms[2, yl] = adam_sum(1, NX - 1)
    for k in range(1, NL):
        adam_copy(2, yl, in_group((yl + k) % NL, c, x)).start()
    for k in range(NL):
        g_late(k)
    adam_total = adam_sum(2, NL - 1)

    def precond_half(s):
        high, low = split(grad[s].reshape(grad_hi.shape[1:]))
        grad_hi[s] = high
        grad_lo[s] = low
        wide = dot(lroot_both, high)
        mixed = wide[:chip_rows] + (wide[chip_rows:] + dot(lroot_hi, low))
        mixed_hi, mixed_lo = split(mixed)
        span = pl.ds(pl.multiple_of(s * half, half), half)
        wide = dot(jnp.concatenate([mixed_hi, mixed_lo], axis=0), rroot_hi[span])
        return wide[:chip_rows] + (wide[chip_rows:] + dot(mixed_hi, rroot_lo[span]))

    precond[...] = precond_half(c).reshape(precond.shape)
    g_finish()
    chip_precond = precond[...].reshape(chip_rows, 2 * half) + precond_half(1 - c)
    precond[...] = chip_precond.reshape(precond.shape)

    norms[yl] = jnp.broadcast_to(sum_all(chip_precond * chip_precond), (1, lanes))
    for k in (3, 2, 1):
        yl_to = (yl, yl + 1 - 2 * (yl % 2), (yl + 2) % NL, NL - 1 - yl)[k]
        remote(norms.at[yl], norms.at[yl], norm_send, norm_recv, in_group(yl_to, c, x)).start()

    own = jnp.concatenate([grad[0, yl, c, x], grad[1, yl, c, x]], axis=1)
    moment_out[0] = 0.99 * moments[c] + 0.01 * own * own

    def times_grad(value):
        rows = value.shape[0]
        high, low = split(value)
        both = jnp.concatenate([high, low], axis=0)
        out = []
        for s in range(2):
            wide = dot(both, grad_hi[s])
            out.append(wide[:rows] + (wide[rows:] + dot(high, grad_lo[s])))
        return jnp.concatenate(out, axis=1)

    own_hi, own_lo = split(own)
    both = jnp.concatenate([own_hi, own_lo], axis=0)
    outer = 0.95 * left_ref[0]
    for s in range(2):
        span = slice(s * half, (s + 1) * half)
        wide = dot_nt(both[:, span], grad_hi[s])
        outer = outer + (wide[:count] + (wide[count:] + dot_nt(own_hi[:, span], grad_lo[s])))
    left_out[0] = outer

    others = norms.at[pl.ds(0, NL - 1)]
    remote(others, others, norm_send, norm_recv, sibling).wait()
    precond_total = jnp.sum(norms[...], axis=0)
    scale = jnp.sqrt(adam_total[:, 0:1]) / (jnp.sqrt(precond_total[:, 0:1]) + 1e-06)
    updates[dp] = (scale * precond[c * NX + x]).astype(BF16)

    def update_copy(d, k, device):
        return remote(updates.at[d], updates.at[d], update_send.at[k], update_recv.at[d], device)

    across = z * 2 + (1 - yh)
    update_sent = [update_copy(dp, 0, at_yz((1 - yh) * NL + yl, z))]
    for k in FAR_FIRST:
        update_sent.append(update_copy(dp, k, at_yz(y, (z + k) % NZ)))
    for copy in update_sent:
        copy.start()
    update_copy(across, 0, sibling).wait_recv()
    for k in FAR_FIRST:
        copy = update_copy(across, NZ - 1 + k, at_yz(y, (z + k) % NZ))
        copy.start()
        update_sent.append(copy)
    pending.extend(update_sent)

    first = seq * (NX * count) + x * count
    lane = 128
    side = first // half
    tile = grad_hi.shape[1]
    strip = grad[side, :, :, :, :, pl.ds(pl.multiple_of((first % half) // lane * lane, lane), lane)]
    columns[...] = strip.reshape(tile, lane).T
    picked = columns[pl.ds(pl.multiple_of(first % lane, count), count)]
    right_out[0] = 0.95 * right_ref[0] + times_grad(picked)

    for k in range(1, NZ):
        for side_y in range(2):
            update_copy(((z + k) % NZ) * 2 + side_y, 0, sibling).wait_recv()
    for copy in pending:
        copy.wait_send()


def deliver(owner_ref, updates, left, right, moment, update_out, left_out, right_out, moment_out):
    for b in range(owner_ref.shape[0]):
        update_out[b] = updates[owner_ref[b]]
    left_out[...] = left[...]
    right_out[...] = right[...]
    moment_out[...] = moment[...]


def per_device(
    activations, d_logits, block_owner, left_stat, right_stat, second_moment, left_root, right_root
):
    tokens, width = activations.shape
    blocks = block_owner.shape[0]
    half = width // 2
    rows = left_stat.shape[1]
    unit = 2 * rows
    vmem = pl.BlockSpec(memory_space=pltpu.VMEM)
    smem = pl.BlockSpec(memory_space=pltpu.SMEM)
    dma = pltpu.SemaphoreType.DMA
    stat = jax.ShapeDtypeStruct(left_stat.shape, F32)
    updates, left, right, moment = pl.pallas_call(
        kernel,
        out_shape=(jax.ShapeDtypeStruct((blocks, rows, width), BF16), stat, stat, stat),
        in_specs=[smem] + [pl.BlockSpec(memory_space=pltpu.HBM)] * 7,
        out_specs=(vmem,) * 4,
        scratch_shapes=[
            pltpu.SMEM((blocks,), jnp.int32),
            pltpu.VMEM((tokens, width), BF16),
            pltpu.VMEM(left_stat.shape, F32),
            pltpu.VMEM(left_stat.shape, F32),
            pltpu.VMEM((2, rows, width), F32),
            pltpu.VMEM((2, NX, rows, width), F32),
            pltpu.VMEM((blocks, tokens, d_logits.shape[1] // blocks), BF16),
            pltpu.VMEM((blocks, tokens, d_logits.shape[1] // blocks), BF16),
            pltpu.VMEM((tokens, half), BF16),
            pltpu.VMEM((64, unit, half), F32),
            pltpu.VMEM((2, 4, 8, unit, half), F32),
            pltpu.VMEM((8, unit, half), F32),
            pltpu.VMEM((2, NL, 2, NX, rows, half), F32),
            pltpu.VMEM((NL, 2, NX, rows, width), F32),
            pltpu.VMEM((2, width, half), BF16),
            pltpu.VMEM((2, width, half), BF16),
            pltpu.VMEM((width, width), BF16),
            pltpu.VMEM((width, width), BF16),
            pltpu.VMEM((128, width), F32),
            pltpu.VMEM((2 * NX, rows, width), F32),
            pltpu.VMEM((3, NX, 1, 128), F32),
            pltpu.VMEM((NL, 1, 128), F32),
            dma((7,)), dma((3,)), dma((3,)),
            dma((2, 4, PIECES)), dma((2, 4, PIECES)),
            dma((8,)), dma((8,)),
            dma((2, 24)), dma((2, 2, NL, NX)),
            dma((4,)), dma((2, NX)),
            dma((3,)), dma((3,)),
            dma, dma,
            dma((15,)), dma((16,)),
        ],
        compiler_params=pltpu.CompilerParams(
            collective_id=0, has_side_effects=True, vmem_limit_bytes=60 * 2**20
        ),
    )(block_owner, activations, d_logits, left_stat, right_stat, second_moment, left_root, right_root)
    return pl.pallas_call(
        deliver,
        out_shape=(jax.ShapeDtypeStruct(updates.shape, BF16), stat, stat, stat),
        in_specs=[smem] + [vmem] * 4,
        out_specs=(vmem,) * 4,
    )(block_owner, updates, left, right, moment)


def solution(mesh):
    shards = P("dp", ("seq", "tensor"), None)
    return jax.shard_map(
        per_device,
        mesh=mesh,
        in_specs=(P(("dp", "seq"), None), P(("dp", "seq"), "tensor"), P()) + (shards,) * 5,
        out_specs=(P(None, ("seq", "tensor"), None), shards, shards, shards),
        check_vma=False,
    )
```

```python
import jax
import jax.numpy as jnp
from jax import lax
from jax.experimental import pallas as pl
from jax.experimental.pallas import tpu as pltpu
from jax.sharding import PartitionSpec as P

F32 = jnp.float32
BF16 = jnp.bfloat16
MESH = pl.DeviceIdType.MESH

NZ = 8
NY = 8
NL = 4
NX = 4
PIECES = 4
FAR_FIRST = (4, 3, 5, 2, 6, 1, 7)
PIECE_ORDER = ((2, 3, 0, 1), (0, 1, 2, 3))


def split(value):
    high = value.astype(BF16)
    return high, (value - high.astype(F32)).astype(BF16)


def dot(a, b):
    return jnp.dot(a, b, preferred_element_type=F32)


def dot_nt(a, b):
    return lax.dot_general(a, b, (((1,), (1,)), ((), ())), preferred_element_type=F32)


def dot_tn(a, b):
    return lax.dot_general(a, b, (((0,), (0,)), ((), ())), preferred_element_type=F32)


def sum_all(value):
    return jnp.sum(jnp.sum(value, axis=0, keepdims=True), axis=1, keepdims=True)


def kernel(
    owner_ref, acts_hbm, logit_ref, left_hbm, right_hbm, moment_hbm, lroot_hbm, rroot_hbm,
    updates, left_out, right_out, moment_out,
    owned_ref, acts_ref, left_ref, right_ref, moments, lroots, logit_own, logit_other, acts_other, part, ring_in, axis_in, grad, rroot, grad_hi, grad_lo,
    rroot_hi, rroot_lo, columns, precond, adam_norms, norms,
    load_done, ex_send, ex_recv, ring_send, ring_recv, axis_send, axis_recv, gather_send, gather_recv,
    lroot_send, lroot_recv, adam_send, adam_recv, norm_send, norm_recv, update_send, update_recv,
):
    dp = lax.axis_index("dp")
    seq = lax.axis_index("seq")
    x = lax.axis_index("tensor")
    z, yh = dp // 2, dp % 2
    yl, c = seq // 2, seq % 2
    y = yh * NL + yl
    half = acts_ref.shape[1] // 2
    pending = []

    def at_yz(y_to, z_to):
        return (z_to * 2 + y_to // NL, (y_to % NL) * 2 + c, x)

    def in_group(yl_to, c_to, x_to):
        return (dp, yl_to * 2 + c_to, x_to)

    sibling = in_group(yl, 1 - c, x)
    i = (1 - c) * z + c * y
    me2 = (1 - c) * y + c * z

    def on_first(k):
        return at_yz((1 - c) * y + c * k, (1 - c) * k + c * z)

    def on_second(k):
        return at_yz((1 - c) * k + c * y, (1 - c) * z + c * k)

    ring_next = on_first((i + 1) % 8)
    ring_prev = on_first((i + 7) % 8)
    x_next, x_prev, x_far = (x + 1) % NX, (x + 3) % NX, (x + 2) % NX

    acts_load = pltpu.make_async_copy(acts_hbm, acts_ref, load_done.at[1])
    rroot_load = pltpu.make_async_copy(rroot_hbm.at[0], rroot.at[yl, c, x], load_done.at[2])
    stat_loads = [
        pltpu.make_async_copy(source, target, load_done.at[3 + k])
        for k, (source, target) in enumerate(
            ((left_hbm, left_ref), (right_hbm, right_ref), (moment_hbm.at[0], moments.at[c]))
        )
    ]
    lroot_load = pltpu.make_async_copy(lroot_hbm.at[0], lroots.at[c, x], load_done.at[6])
    rroot_load.start()
    acts_load.start()
    lroot_load.start()
    blocks = owner_ref.shape[0]
    band = logit_ref.shape[1] // blocks
    for b in range(blocks):
        pltpu.make_async_copy(logit_ref.at[:, pl.ds(b * band, band)], logit_own.at[b], load_done.at[0]).start()

    for load in stat_loads:
        load.start()

    barrier = pltpu.get_barrier_semaphore()

    def signal(device):
        pl.semaphore_signal(barrier, inc=1, device_id=device, device_id_type=MESH)

    partners = [at_yz((1 - yh) * NL + k, z) for k in range(NL)]
    partners += [at_yz(y, (z + k) % NZ) for k in FAR_FIRST]
    partners += [in_group((yl + k) % NL, c, x) for k in range(1, NL)]
    partners += [in_group(yl, c, column) for column in (x_far, x_next, x_prev)] + [sibling]
    for device in partners:
        signal(device)
    pl.semaphore_wait(barrier, len(partners))

    def remote(src, dst, send, recv, device):
        return pltpu.make_async_remote_copy(
            src_ref=src, dst_ref=dst, send_sem=send, recv_sem=recv,
            device_id=device, device_id_type=MESH,
        )

    exchange = [
        remote(
            acts_hbm.at[:, pl.ds(pl.multiple_of((1 - c) * half, half), half)],
            acts_other, ex_send.at[0], ex_recv.at[0], sibling,
        )
    ]
    exchange[0].start()
    for b in range(blocks):
        strip = logit_ref.at[:, pl.ds(b * band, band)]
        remote(strip, logit_other.at[b], ex_send.at[1], ex_recv.at[1], sibling).start()
    exchange.append(remote(moment_hbm.at[0], moments.at[c], ex_send.at[2], ex_recv.at[2], sibling))
    exchange[1].start()
    exchange.append(remote(logit_other, logit_other, ex_send.at[1], ex_recv.at[1], sibling))

    def gather(which, slab, band_of):
        count = [0]

        def describe(place, k, core, q, column, device):
            return remote(
                place, place, gather_send.at[which, k], gather_recv.at[which, core, q, column], device
            )

        def arrive(q, column):
            describe(slab(q, c, column), 0, c, q, column, sibling).wait_recv()

        def launch(place, q, column, device):
            copy = describe(place, count[0], c, q, column, device)
            count[0] += 1
            copy.start()
            pending.append(copy)

        def push(q, column, device):
            launch(slab(q, c, column), q, column, device)

        def share(q):
            launch(band_of(q, c), q, 0, sibling)

        columns_to = [in_group(yl, c, column) for column in (x_far, x_next, x_prev)]

        def around(k):
            return (yl, yl + 1 - 2 * (yl % 2), (yl + 2) % NL, NL - 1 - yl)[k]

        def begin():
            for k in (3, 2, 1):
                push(yl, x, in_group(around(k), c, x))
            for device in columns_to:
                push(yl, x, device)

        def middle():
            for k in (1, 2, 3):
                arrive(around(k), x)
                for device in columns_to:
                    push(around(k), x, device)

        def late(k):
            for column in (x_next, x_prev, x_far):
                arrive(around(k), column)
            share(around(k))

        def finish():
            for q in range(NL):
                describe(band_of(q, 1 - c), 0, 1 - c, q, 0, sibling).wait_recv()

        return begin, middle, late, finish

    rroot_load.wait()
    r_begin, r_middle, r_late, r_finish = gather(
        0, lambda q, core, column: rroot.at[q, core, column], lambda q, core: rroot.at[q, core]
    )
    g_begin, g_middle, g_late, g_finish = gather(
        1, lambda q, core, column: grad.at[core, q, :, column], lambda q, core: grad.at[core, q]
    )

    def lroot_copy(k, column, device):
        return remote(
            lroots.at[c, column], lroots.at[c, column], lroot_send.at[k], lroot_recv.at[0, column], device
        )

    def lroot_band(core):
        return remote(lroots.at[core], lroots.at[core], lroot_send.at[3], lroot_recv.at[1, 0], sibling)

    unit = band // NL

    def place(d, q):
        row = (d % 2) * NL + q
        return (1 - c) * ((d // 2) * 8 + row) + c * (row * 8 + d // 2)

    def ordered(n):
        return (1 - c) * ((2 * (i + 4) + n) % 16) + c * (2 * (n % 8) + (yh + 1 + n // 8) % 2)

    def own_block(d, carry):
        b = jnp.int32(0)
        for k in range(1, blocks):
            apart = owner_ref[k] - d
            b = b + k * lax.shift_right_logical(blocks * blocks - apart * apart, jnp.int32(8))
        b = lax.rem(b, jnp.int32(blocks))
        owned_ref[d] = b
        rows = dot_tn(logit_own[b], acts_own)
        for q in range(NL):
            part[place(d, q)] = rows[q * unit : (q + 1) * unit]
        return carry

    pltpu.make_async_copy(logit_own, logit_own, load_done.at[0]).wait()
    acts_load.wait()
    acts_own = acts_ref[:, pl.ds(pl.multiple_of(c * half, half), half)]
    lax.fori_loop(0, blocks, own_block, 0, unroll=4)
    r_begin()
    lroot_load.wait()
    for k, column in enumerate((x_far, x_next, x_prev)):
        copy = lroot_copy(k, x, in_group(yl, c, column))
        copy.start()
        pending.append(copy)

    for copy in exchange:
        copy.wait_recv()
    pending.extend(exchange)

    acts_rest = acts_other[...]

    def other_block(n, carry):
        d = ordered(n)
        rows = dot_tn(logit_other[owned_ref[d]], acts_rest)
        for q in range(NL):
            spot = place(d, q)
            part[spot] = part[spot] + rows[q * unit : (q + 1) * unit]
        return carry


    def chunk(way, step):
        return (i + 4 - step) % 8 if way == 0 else (i + 4 + step) % 8

    def ring(way, step, piece):
        return remote(
            part.at[pl.ds(chunk(way, step) * 8 + 2 * piece, 2)],
            ring_in.at[way, step, pl.ds(2 * piece, 2)],
            ring_send.at[way, step, piece], ring_recv.at[way, step, piece],
            (ring_next, ring_prev)[way],
        )

    def first_pieces(way):
        return (0, 1) if way == 0 else (2, 3)

    def ring_add(spot, way, step, piece):
        ring(way, step, piece).wait_recv()
        rows = pl.ds(spot * 8 + 2 * piece, 2)
        part[rows] = part[rows] + ring_in[way, step, pl.ds(2 * piece, 2)]

    def ring_send_off(way, step, piece):
        copy = ring(way, step, piece)
        copy.start()
        pending.append(copy)

    lax.fori_loop(0, blocks // 2, other_block, 0, unroll=4)
    for k in range(2):
        for way in range(2):
            ring_send_off(way, 0, first_pieces(way)[k])
    lax.fori_loop(blocks // 2, blocks, other_block, 0, unroll=4)
    for k in range(2):
        for way in range(2):
            ring_send_off(way, 1, PIECE_ORDER[way][k])
    r_middle()
    for step in range(1, 4):
        if step == 2:
            pass
        for k in range(PIECES):
            for way in range(2):
                piece = PIECE_ORDER[way][k]
                if step == 1 and k < 2:
                    continue
                ring_add(chunk(way, step), way, step - 1, piece)
                ring_send_off(way, step, piece)

    def axis_copy(j):
        return remote(
            part.at[i * 8 + j], axis_in.at[me2], axis_send.at[j], axis_recv.at[me2], on_second(j)
        )

    for k in range(PIECES):
        for way in range(2):
            ring_add(i, way, 3, PIECE_ORDER[way][k])
        for piece in {2: (0, 2), 3: (1, 3)}.get(k, ()):
            for j in (2 * piece, 2 * piece + 1):

                @pl.when(j != me2)
                def _():
                    axis_copy(j).start()

    for k in range(1, 8):
        pending.append(axis_copy((me2 + k) % 8))
    for k in range(NL):
        r_late(k)
    for column in (x_next, x_prev, x_far):
        lroot_copy(0, column, sibling).wait_recv()
    copy = lroot_band(c)
    copy.start()
    pending.append(copy)
    r_finish()
    lroot_band(1 - c).wait_recv()
    value = rroot[...].reshape(rroot_hi.shape)
    rroot_hi[...], rroot_lo[...] = split(value)

    total = part[i * 8 + me2]
    for k in range(1, 8):
        j = (me2 + k) % 8
        remote(part.at[i * 8 + j], axis_in.at[j], axis_send.at[j], axis_recv.at[j], sibling).wait_recv()
        total = total + axis_in[j]
    grad[c, yl, :, x] = total.reshape(2, unit // 2, half)

    g_begin()
    for load in stat_loads:
        load.wait()

    slab_grad = total.reshape(2, unit // 2, half)
    slab_moment = moments[:, :, pl.ds(pl.multiple_of(c * half, half), half)]
    slab_adam = slab_grad / (jnp.sqrt(0.99 * slab_moment + 0.01 * slab_grad * slab_grad) + 1e-08)
    lanes = norms.shape[2]

    def adam_copy(level, place, device):
        spot = adam_norms.at[level, place]
        return remote(spot, spot, adam_send.at[level], adam_recv.at[level], device)

    def adam_sum(level, others):
        several = adam_norms.at[level, pl.ds(0, others)]
        remote(several, several, adam_send.at[level], adam_recv.at[level], sibling).wait()
        return jnp.sum(adam_norms[level, 0 : others + 1], axis=0)

    adam_norms[0, c] = jnp.broadcast_to(sum_all((slab_adam * slab_adam).reshape(unit, half)), (1, lanes))
    adam_copy(0, c, sibling).start()
    count = lroots.shape[2]
    chip_rows = lroots.shape[0] * lroots.shape[1] * count
    lroot_hi, lroot_lo = split(lroots[...].reshape(chip_rows, lroots.shape[3]))
    lroot_both = jnp.concatenate([lroot_hi, lroot_lo], axis=0)
    adam_norms[1, x] = adam_sum(0, 1)
    for column in (x_far, x_next, x_prev):
        adam_copy(1, x, in_group(yl, c, column)).start()
    g_middle()
    adam_norms[2, yl] = adam_sum(1, NX - 1)
    for k in range(1, NL):
        adam_copy(2, yl, in_group((yl + k) % NL, c, x)).start()
    for k in range(NL):
        g_late(k)
    adam_total = adam_sum(2, NL - 1)

    def precond_half(s):
        high, low = split(grad[s].reshape(grad_hi.shape[1:]))
        grad_hi[s] = high
        grad_lo[s] = low
        wide = dot(lroot_both, high)
        mixed = wide[:chip_rows] + (wide[chip_rows:] + dot(lroot_hi, low))
        mixed_hi, mixed_lo = split(mixed)
        span = pl.ds(pl.multiple_of(s * half, half), half)
        wide = dot(jnp.concatenate([mixed_hi, mixed_lo], axis=0), rroot_hi[span])
        return wide[:chip_rows] + (wide[chip_rows:] + dot(mixed_hi, rroot_lo[span]))

    precond[...] = precond_half(c).reshape(precond.shape)
    g_finish()
    chip_precond = precond[...].reshape(chip_rows, 2 * half) + precond_half(1 - c)

    norms[yl] = jnp.broadcast_to(sum_all(chip_precond * chip_precond), (1, lanes))
    for k in (3, 2, 1):
        yl_to = (yl, yl + 1 - 2 * (yl % 2), (yl + 2) % NL, NL - 1 - yl)[k]
        remote(norms.at[yl], norms.at[yl], norm_send, norm_recv, in_group(yl_to, c, x)).start()

    precond[...] = chip_precond.reshape(precond.shape)
    own = jnp.concatenate([grad[0, yl, c, x], grad[1, yl, c, x]], axis=1)
    moment_out[0] = 0.99 * moments[c] + 0.01 * own * own

    def times_grad(value):
        rows = value.shape[0]
        high, low = split(value)
        both = jnp.concatenate([high, low], axis=0)
        out = []
        for s in range(2):
            wide = dot(both, grad_hi[s])
            out.append(wide[:rows] + (wide[rows:] + dot(high, grad_lo[s])))
        return jnp.concatenate(out, axis=1)

    own_hi, own_lo = split(own)
    both = jnp.concatenate([own_hi, own_lo], axis=0)
    outer = 0.95 * left_ref[0]
    for s in range(2):
        span = slice(s * half, (s + 1) * half)
        wide = dot_nt(both[:, span], grad_hi[s])
        outer = outer + (wide[:count] + (wide[count:] + dot_nt(own_hi[:, span], grad_lo[s])))
    left_out[0] = outer

    others = norms.at[pl.ds(0, NL - 1)]
    remote(others, others, norm_send, norm_recv, sibling).wait()
    precond_total = jnp.sum(norms[...], axis=0)
    scale = jnp.sqrt(adam_total[:, 0:1]) / (jnp.sqrt(precond_total[:, 0:1]) + 1e-06)
    updates[dp] = (scale * precond[c * NX + x]).astype(BF16)

    def update_copy(d, k, device):
        return remote(updates.at[d], updates.at[d], update_send.at[k], update_recv.at[d], device)

    across = z * 2 + (1 - yh)
    update_sent = [update_copy(dp, 0, at_yz((1 - yh) * NL + yl, z))]
    for k in FAR_FIRST:
        update_sent.append(update_copy(dp, k, at_yz(y, (z + k) % NZ)))
    for copy in update_sent:
        copy.start()
    update_copy(across, 0, sibling).wait_recv()
    for k in FAR_FIRST:
        copy = update_copy(across, NZ - 1 + k, at_yz(y, (z + k) % NZ))
        copy.start()
        update_sent.append(copy)
    pending.extend(update_sent)

    first = seq * (NX * count) + x * count
    lane = 128
    side = first // half
    tile = grad_hi.shape[1]
    strip = grad[side, :, :, :, :, pl.ds(pl.multiple_of((first % half) // lane * lane, lane), lane)]
    columns[...] = strip.reshape(tile, lane).T
    picked = columns[pl.ds(pl.multiple_of(first % lane, count), count)]
    right_out[0] = 0.95 * right_ref[0] + times_grad(picked)

    for k in range(1, NZ):
        for side_y in range(2):
            update_copy(((z + k) % NZ) * 2 + side_y, 0, sibling).wait_recv()
    for copy in pending:
        copy.wait_send()


def deliver(owner_ref, updates, left, right, moment, update_out, left_out, right_out, moment_out):
    for b in range(owner_ref.shape[0]):
        update_out[b] = updates[owner_ref[b]]
    left_out[...] = left[...]
    right_out[...] = right[...]
    moment_out[...] = moment[...]


def per_device(
    activations, d_logits, block_owner, left_stat, right_stat, second_moment, left_root, right_root
):
    tokens, width = activations.shape
    blocks = block_owner.shape[0]
    half = width // 2
    rows = left_stat.shape[1]
    unit = 2 * rows
    vmem = pl.BlockSpec(memory_space=pltpu.VMEM)
    smem = pl.BlockSpec(memory_space=pltpu.SMEM)
    dma = pltpu.SemaphoreType.DMA
    stat = jax.ShapeDtypeStruct(left_stat.shape, F32)
    updates, left, right, moment = pl.pallas_call(
        kernel,
        out_shape=(jax.ShapeDtypeStruct((blocks, rows, width), BF16), stat, stat, stat),
        in_specs=[smem] + [pl.BlockSpec(memory_space=pltpu.HBM)] * 7,
        out_specs=(vmem,) * 4,
        scratch_shapes=[
            pltpu.SMEM((blocks,), jnp.int32),
            pltpu.VMEM((tokens, width), BF16),
            pltpu.VMEM(left_stat.shape, F32),
            pltpu.VMEM(left_stat.shape, F32),
            pltpu.VMEM((2, rows, width), F32),
            pltpu.VMEM((2, NX, rows, width), F32),
            pltpu.VMEM((blocks, tokens, d_logits.shape[1] // blocks), BF16),
            pltpu.VMEM((blocks, tokens, d_logits.shape[1] // blocks), BF16),
            pltpu.VMEM((tokens, half), BF16),
            pltpu.VMEM((64, unit, half), F32),
            pltpu.VMEM((2, 4, 8, unit, half), F32),
            pltpu.VMEM((8, unit, half), F32),
            pltpu.VMEM((2, NL, 2, NX, rows, half), F32),
            pltpu.VMEM((NL, 2, NX, rows, width), F32),
            pltpu.VMEM((2, width, half), BF16),
            pltpu.VMEM((2, width, half), BF16),
            pltpu.VMEM((width, width), BF16),
            pltpu.VMEM((width, width), BF16),
            pltpu.VMEM((128, width), F32),
            pltpu.VMEM((2 * NX, rows, width), F32),
            pltpu.VMEM((3, NX, 1, 128), F32),
            pltpu.VMEM((NL, 1, 128), F32),
            dma((7,)), dma((3,)), dma((3,)),
            dma((2, 4, PIECES)), dma((2, 4, PIECES)),
            dma((8,)), dma((8,)),
            dma((2, 24)), dma((2, 2, NL, NX)),
            dma((4,)), dma((2, NX)),
            dma((3,)), dma((3,)),
            dma, dma,
            dma((15,)), dma((16,)),
        ],
        compiler_params=pltpu.CompilerParams(
            collective_id=0, has_side_effects=True, vmem_limit_bytes=60 * 2**20
        ),
    )(block_owner, activations, d_logits, left_stat, right_stat, second_moment, left_root, right_root)
    return pl.pallas_call(
        deliver,
        out_shape=(jax.ShapeDtypeStruct(updates.shape, BF16), stat, stat, stat),
        in_specs=[smem] + [vmem] * 4,
        out_specs=(vmem,) * 4,
    )(block_owner, updates, left, right, moment)


def solution(mesh):
    shards = P("dp", ("seq", "tensor"), None)
    return jax.shard_map(
        per_device,
        mesh=mesh,
        in_specs=(P(("dp", "seq"), None), P(("dp", "seq"), "tensor"), P()) + (shards,) * 5,
        out_specs=(P(None, ("seq", "tensor"), None), shards, shards, shards),
        check_vma=False,
    )
```
